32 devices in a mesh: section: 8 (over z, y), expert: 4 (over x, core).
Axes of the slice: x: 2, y: 2, z: 4, core: 2. Of those that a mesh axis runs over, the one named last changes fastest.
Arguments:
- tokens: bfloat16 [8, 512, 3584], P('section', 'expert'), may hold values from -6 to 6
- norm_gain: float32 [8, 3584], P('section'), may hold values from 0.1 to 1.9
- expert_ids: int32 [8, 512, 2], P('section', 'expert'), may hold values from 0 to 3, all different within a row; in each aligned block of 128 rows (0 to 127, 128 to 255, ..., all dimensions but the last counted through in order) at most 80 rows name the same one
- gate_values: float32 [8, 512, 2], P('section', 'expert'), may hold values from 0.2 to 1
- gate_weight: bfloat16 [8, 3584, 8192], P('section', None, 'expert'), may hold values from -0.09375 to 0.09375
- up_weight: bfloat16 [8, 3584, 8192], P('section', None, 'expert'), may hold values from -0.09375 to 0.09375
- down_weight: bfloat16 [8, 8192, 3584], P('section', 'expert'), may hold values from -0.125 to 0.125
Outputs:
- handed: bfloat16 [8, 512, 3584], P('section', 'expert')
The draws below stay inside these ranges and needn't reach their ends.
Inputs may be any that keep to these rules, and one draw needn't show every extreme that they name: `expert_ids`: each token names 2 different experts. Of the 128 tokens of one device (aligned blocks of 128 rows), at most 80 choose any one expert, and exactly 80 choose some expert in some blocks.
All inputs are finite; a program needn't handle non-finite values.
Results may differ from the reference program's by a relative error of at most 0.0053.
Values may be sent and summed in bfloat16 or wider, within the bound.
A program may use at most 128 MiB of HBM per device.

```python
import math
import jax
import jax.numpy as jnp
import numpy as np
from jax import lax

D = 3584
FF = 2048
EXPERTS = 4
TOP = 2
TOK_DEV = 128
CAP = 80
MB = 512
N_SECTION = 8
N_EXPERT = 4


def steps_of(rng, extent, split, least, high):
    def one(position, blocks):
        steps = jax.random.uniform(jax.random.fold_in(jax.random.fold_in(rng, 6), position), (blocks,), jnp.float32, least / len(split), high / len(split))
        return jnp.repeat(jnp.exp(steps), extent[position] // blocks).reshape((-1,) + (1,) * (len(extent) - position - 1))

    level = one(*split[0])
    for cut in split[1:]:
        level = level * one(*cut)
    return level


def shared_out(key, own, number, rows, count, top, bound, slope):
    sequence = jax.random.permutation(key, count)
    heavy_load, ordinary = shares(count, rows * top, bound, slope, True), shares(count, rows * top, bound, slope, False)
    places = jnp.arange(count)

    def named(tallies, rotation):
        used = int((tallies > 0).sum())
        fixed = max(1, used // 4)
        shifted = fixed + (places - fixed + rotation * (used - fixed)) % max(1, count - fixed)
        return jnp.zeros((count,), jnp.int32).at[sequence[jnp.where(places < fixed, places, shifted)]].set(jnp.asarray(tallies, jnp.int32))

    tallies = jnp.where(number % 4 == 0, named(heavy_load, number // 4), named(ordinary, number - number // 4 - 1))
    mixed = jax.random.permutation(jax.random.fold_in(own, 3), count)
    source_of, receiver = mixed[0:count // 2 * 2:2], mixed[1:count // 2 * 2:2]
    room = jnp.minimum(tallies[source_of] - 1, bound - tallies[receiver]) // 2
    room = jnp.where((source_of == sequence[0]) | (receiver == sequence[0]) | (tallies[receiver] == 0), 0, jnp.maximum(room, 0))
    shifted = jax.random.randint(jax.random.fold_in(own, 4), (count // 2,), 0, 1 << 20) % (room + 1)
    tallies = tallies.at[source_of].add(-shifted).at[receiver].add(shifted)
    items = jnp.searchsorted(jnp.cumsum(tallies), jnp.arange(rows * top), side="right").astype(jnp.int32)
    grid = items.reshape(top, rows).T
    grid = grid[jax.random.permutation(jax.random.fold_in(own, 1), rows)]
    rotation = jax.random.randint(jax.random.fold_in(own, 2), (rows, 1), 0, top)
    return jnp.take_along_axis(grid, (jnp.arange(top)[None, :] + rotation) % top, axis=1)


def shares(number_of, total, most, skew, full):
    weights = [(1 << 20) // math.isqrt(grade ** skew) + 1 for grade in range(1, number_of + 1)]
    largest = most if full else min(most, max(-(-total // number_of), total * weights[0] // sum(weights)))
    least = 1 if total - largest >= number_of - 1 else 0
    given, spare = [largest] + [least] * (number_of - 1), total - largest - least * (number_of - 1)
    while spare > 0:
        movable = [i for i in range(1, number_of) if given[i] < largest] or [i for i in range(1, number_of) if given[i] < most]
        mass, remaining = sum([weights[i] for i in movable]), spare
        for i in movable:
            addition = min(most - given[i], max(1, remaining * weights[i] // mass), spare)
            given[i] = given[i] + addition
            spare = spare - addition
    return np.array(given)


def normal_values(own_key, shape, scale, bound, split=(), kind=jnp.bfloat16):
    drawn = jax.random.normal(own_key, shape, jnp.float32) * scale
    if len(split) > 0:
        drawn = steps_of(own_key, shape, split, -0.22, 0.18) * drawn
    return jnp.clip(drawn, min=-bound, max=bound).astype(kind)


def setup_inputs(seed: int = 0) -> dict:
    key_of = jax.random.split(jax.random.key(seed), 8)
    tokens = normal_values(key_of[0], (N_SECTION, MB, D), 1.0, 6.0, ((0, 8), (1, 4)))
    norm_gain = jnp.clip(1.0 + 0.18 * jax.random.normal(key_of[1], (N_SECTION, D), jnp.float32), 0.1, 1.9)
    expert_ids_keys = jax.random.split(jax.random.fold_in(key_of[2], 1), N_SECTION * MB // TOK_DEV)
    expert_ids_turns = jax.random.permutation(jax.random.fold_in(key_of[2], 3), N_SECTION * MB // TOK_DEV)
    expert_ids = jax.vmap(lambda own, number: shared_out(jax.random.fold_in(key_of[2], 2), own, number, TOK_DEV, EXPERTS, TOP, CAP, 2))(expert_ids_keys, expert_ids_turns).reshape((N_SECTION, MB, TOP))
    gate_values = jnp.clip(0.2 + 0.8 * jax.random.uniform(key_of[3], (N_SECTION, MB, TOP), jnp.float32) ** steps_of(key_of[3], (N_SECTION, MB, TOP), ((0, 8), (1, 4)), -0.2, 0.2), 0.2, 1.0)
    gate_weight = normal_values(key_of[4], (N_SECTION, D, EXPERTS * FF), D ** -0.5, 0.09375, ((0, 8), (2, 4)))
    up_weight = normal_values(key_of[5], (N_SECTION, D, EXPERTS * FF), D ** -0.5, 0.09375, ((0, 8), (2, 4)))
    down_weight = normal_values(key_of[6], (N_SECTION, EXPERTS * FF, D), FF ** -0.5, 0.125, ((0, 8), (1, 4)))
    return {"tokens": tokens, "norm_gain": norm_gain, "expert_ids": expert_ids, "gate_values": gate_values, "gate_weight": gate_weight, "up_weight": up_weight, "down_weight": down_weight}


def expert_layer(resident, norm_gain, expert_ids, gate_values, gate_weight, up_weight, down_weight):
    shards = N_EXPERT // EXPERTS
    units = FF // shards
    limit = N_EXPERT * CAP
    widened = resident.astype(jnp.float32)
    scale = lax.rsqrt(lax.optimization_barrier(jnp.mean(widened * widened, axis=-1, keepdims=True)) + 1e-06)
    normed = (widened * scale * norm_gain.astype(jnp.float32)).astype(jnp.bfloat16)
    mixture = jnp.zeros(widened.shape, jnp.float32)
    for expert in range(EXPERTS):
        matches = expert_ids == expert
        chosen = jnp.any(matches, axis=-1)
        weight = lax.optimization_barrier(jnp.sum(jnp.where(matches, gate_values, jnp.zeros_like(gate_values)), axis=-1))
        picking = jnp.argsort(1 - chosen.astype(jnp.int32), stable=True)[:limit]
        routed = normed[picking]
        first = expert * FF
        gate = jnp.dot(routed, gate_weight[:, first:first + FF], preferred_element_type=jnp.float32)
        upward = jnp.dot(routed, up_weight[:, first:first + FF], preferred_element_type=jnp.float32)
        hidden = (jax.nn.silu(gate) * upward).astype(jnp.bfloat16)
        pieces = jnp.einsum('rsu,sud->rsd', hidden.astype(jnp.float32).reshape(limit, shards, units), down_weight[first:first + FF].astype(jnp.float32).reshape(shards, units, D))
        rounded = lax.optimization_barrier(pieces.astype(jnp.bfloat16)).astype(jnp.float32)
        summed = lax.optimization_barrier(jnp.sum(rounded, axis=1))
        mixture = mixture.at[picking].add(weight[picking][:, None] * summed)
    return (widened + mixture).astype(jnp.bfloat16)

def reference(tokens, norm_gain, expert_ids, gate_values, gate_weight, up_weight, down_weight):

    def one_section(parts):
        return expert_layer(*parts)
    outputs = lax.map(one_section, (tokens, norm_gain, expert_ids, gate_values, gate_weight, up_weight, down_weight))
    return jnp.roll(outputs, 1, axis=0)
```

```python
import functools

import jax
import jax.numpy as jnp
from jax import lax
from jax.experimental import pallas as pl
from jax.experimental.pallas import tpu as pltpu
from jax.sharding import PartitionSpec as P

EXPERTS = 4
TOP = 2
CAP = 80
MESH = pl.DeviceIdType.MESH
F32 = jnp.float32
BF16 = jnp.bfloat16
UP_CHUNKS = 4
WIDE = 512
NARROW = 256
STEP = 16


def kernel(
    sections, tok, gain, ids, gates, gate_hbm, up_hbm, down_hbm, out,
    gate_w, up_w, down_w, nrm, meta, pick, scale, rows_in, hidden, base, local_out, local_in,
    far_out, far_in, back,
    w_sem, meta_s, meta_r, sib_s, sib_r, x_s, x_r, relay_s, relay_r, local_s, local_r,
    swap_s, swap_r, back_s, back_r, hand_s, hand_r,
):
    tokens, model = tok.shape
    units = gate_w.shape[1]
    half = tokens // 2
    steps = half // STEP
    section = lax.axis_index("section")
    me = lax.axis_index("expert")
    chip = lax.div(me, 2)
    core = lax.rem(me, 2)
    other = 1 - core
    sibling = chip * 2 + other
    far_chip = (1 - chip) * 2
    after = lax.rem(section + 1, sections)
    before = lax.rem(section + sections - 1, sections)
    mine = pl.ds(pl.multiple_of(core * half, half), half)
    theirs = pl.ds(pl.multiple_of(other * half, half), half)

    def remote(src, dst, send, recv, **device):
        return pltpu.make_async_remote_copy(
            src_ref=src, dst_ref=dst, send_sem=send, recv_sem=recv,
            device_id=device, device_id_type=MESH,
        )

    barrier = pltpu.get_barrier_semaphore()
    for peer in (sibling, far_chip, far_chip + 1):
        pl.semaphore_signal(barrier, inc=1, device_id={"expert": peer}, device_id_type=MESH)
    for peer in (after, before):
        pl.semaphore_signal(barrier, inc=1, device_id={"section": peer}, device_id_type=MESH)

    up_width = units // UP_CHUNKS

    def gate_copy(k):
        cols = pl.ds(pl.multiple_of(k * up_width, up_width), up_width)
        return pltpu.make_async_copy(gate_hbm.at[:, cols], gate_w.at[:, cols], w_sem.at[k])

    def up_copy(k):
        cols = pl.ds(pl.multiple_of(k * up_width, up_width), up_width)
        return pltpu.make_async_copy(up_hbm.at[:, cols], up_w.at[:, cols], w_sem.at[UP_CHUNKS + k])

    def down_copy(k):
        cols = pl.ds(pl.multiple_of(k * WIDE, WIDE), WIDE)
        return pltpu.make_async_copy(
            down_hbm.at[:, cols], down_w.at[:, cols], w_sem.at[2 * UP_CHUNKS + k]
        )

    for k in range(UP_CHUNKS):
        gate_copy(k).start()
        up_copy(k).start()
    for k in range(model // WIDE):
        down_copy(k).start()

    meta[0] = jnp.zeros(meta.shape[1:], F32)
    meta[0, 0:TOP, :] = ids[...].astype(F32)
    meta[0, TOP:2 * TOP, :] = gates[...]

    @pl.loop(0, tokens // STEP)
    def _(i):
        rows = pl.ds(pl.multiple_of(i * STEP, STEP), STEP)
        widened = tok[rows, :].astype(F32)
        inverse = lax.rsqrt(jnp.mean(widened * widened, axis=-1, keepdims=True) + 1e-06)
        nrm[0, rows, :] = (widened * inverse * gain[...]).astype(BF16)

    pl.semaphore_wait(barrier, 5)

    def sib_copy(k, rows):
        return remote(
            nrm.at[0, rows], nrm.at[1, rows], sib_s.at[k], sib_r.at[k], expert=sibling
        )

    def x_copy(source):
        slot = lax.rem(source + 2 - core, 2)
        return remote(
            nrm.at[slot, mine], nrm.at[2 + source, mine], x_s.at[source], x_r.at[source],
            expert=far_chip + core,
        )

    def relay_copy(source, rows):
        return remote(
            nrm.at[2 + source, rows], nrm.at[2 + source, rows], relay_s.at[source],
            relay_r.at[source], expert=sibling,
        )

    meta_copies = [
        remote(meta.at[0], meta.at[1], meta_s.at[0], meta_r.at[0], expert=sibling),
        remote(meta.at[0], meta.at[2 + core], meta_s.at[1], meta_r.at[1 + core], expert=far_chip),
        remote(
            meta.at[0], meta.at[2 + core], meta_s.at[2], meta_r.at[1 + core], expert=far_chip + 1
        ),
    ]
    sib_copy(0, theirs).start()

    @pl.when(core == 0)
    def _():
        x_copy(0).start()

    for copy in meta_copies:
        copy.start()
    sib_copy(1, mine).start()
    sib_copy(0, mine).wait_recv()

    @pl.when(core == 1)
    def _():
        x_copy(0).start()

    x_copy(1).start()

    def meta_arrived(slot):
        remote(
            meta.at[0], meta.at[slot], meta_s.at[0], meta_r.at[slot - 1], expert=sibling
        ).wait_recv()

    def gather(slot, place):
        expert = me.astype(F32)
        about = meta[slot]
        first = about[0:1, :] == expert
        second = about[1:2, :] == expert
        chosen = jnp.where(first, 1.0, 0.0) + jnp.where(second, 1.0, 0.0)
        weight = jnp.where(first, about[2:3, :], 0.0) + jnp.where(second, about[3:4, :], 0.0)
        upper = jnp.where(
            lax.broadcasted_iota(jnp.int32, (tokens, tokens), 0)
            < lax.broadcasted_iota(jnp.int32, (tokens, tokens), 1),
            1.0, 0.0,
        ).astype(BF16)
        ahead = jnp.dot(
            jnp.broadcast_to(chosen, (16, tokens)).astype(BF16), upper,
            preferred_element_type=F32,
        )[0:1, :]
        wanted = lax.broadcasted_iota(jnp.int32, (CAP, tokens), 0).astype(F32)
        picked = jnp.where(ahead == wanted, 1.0, 0.0) * chosen
        pick[place] = picked.astype(BF16)
        scale[place] = jnp.broadcast_to(
            jnp.sum(picked * weight, axis=1, keepdims=True), (CAP, scale.shape[2])
        )

        @pl.loop(0, model // WIDE)
        def _(n):
            cols = pl.ds(pl.multiple_of(n * WIDE, WIDE), WIDE)
            rows_in[place * CAP:(place + 1) * CAP, cols] = jnp.dot(
                pick[place], nrm[slot, :, cols], preferred_element_type=F32
            ).astype(BF16)

    def up_tile(count, i):
        cols = pl.ds(pl.multiple_of(i * NARROW, NARROW), NARROW)
        gate = jnp.dot(rows_in[0:count, :], gate_w[:, cols], preferred_element_type=F32)
        upward = jnp.dot(rows_in[0:count, :], up_w[:, cols], preferred_element_type=F32)
        hidden[0:count, cols] = (jax.nn.silu(gate) * upward).astype(BF16)

    def spread(place, product):
        weighted = (
            product[place * CAP:(place + 1) * CAP, :] * scale[place][:, 0:1]
        ).astype(BF16)
        return lax.dot_general(
            pick[place], weighted, (((0,), (0,)), ((), ())), preferred_element_type=F32
        )

    def swap_copy(source, rows):
        return remote(
            far_out.at[source, rows], far_in.at[source], swap_s.at[source], swap_r.at[source],
            expert=sibling,
        )

    def back_copy(source, q):
        rows = pl.ds(pl.multiple_of(core * half + q * STEP, STEP), STEP)
        return remote(
            far_out.at[source, rows], back.at[rows], back_s.at[source * steps + q],
            back_r.at[core * steps + q], expert=far_chip + source,
        )

    def send_back(source):
        swap_copy(source, theirs).wait_recv()

        @pl.loop(0, steps)
        def _(q):
            rows = pl.ds(pl.multiple_of(core * half + q * STEP, STEP), STEP)
            near = pl.ds(pl.multiple_of(q * STEP, STEP), STEP)
            far_out[source, rows, :] = (
                far_out[source, rows, :].astype(F32) + far_in[source, near, :].astype(F32)
            ).astype(BF16)
            back_copy(source, q).start()

    def hand_copy(sender, q):
        rows = pl.ds(pl.multiple_of(sender * half + q * STEP, STEP), STEP)
        return remote(
            back.at[rows], out.at[rows], hand_s.at[sender * steps + q],
            hand_r.at[sender * steps + q], section=after,
        )

    def finish(q):
        for sender in range(2):
            rows = pl.ds(pl.multiple_of(sender * half + q * STEP, STEP), STEP)
            remote(
                back.at[rows], back.at[rows], back_s.at[0], back_r.at[sender * steps + q],
                expert=far_chip,
            ).wait_recv()
            total = base[rows, :] + local_in[rows, :].astype(F32) + back[rows, :].astype(F32)
            back[rows, :] = total.astype(BF16)
            hand_copy(sender, q).start()

    local_copy = remote(
        local_out, local_in, local_s.at[0], local_r.at[0], expert=sibling
    )

    gather(0, 0)
    sib_copy(1, theirs).wait_recv()
    meta_arrived(1)
    gather(1, 1)

    @pl.loop(0, UP_CHUNKS)
    def _(k):
        gate_copy(k).wait()
        up_copy(k).wait()

        @pl.loop(0, up_width // NARROW)
        def _(i):
            up_tile(2 * CAP, k * (up_width // NARROW) + i)

    @pl.loop(0, model // WIDE)
    def _(n):
        down_copy(n).wait()
        cols = pl.ds(pl.multiple_of(n * WIDE, WIDE), WIDE)
        product = jnp.dot(hidden[...], down_w[:, cols], preferred_element_type=F32)
        base[:, cols] = tok[:, cols].astype(F32) + spread(0, product)
        local_out[:, cols] = spread(1, product).astype(BF16)

        @pl.when(n == 3)
        def _():
            x_copy(0).wait_recv()
            relay_copy(0, mine).start()

    local_copy.start()

    for source in range(2):
        if source == 1:
            x_copy(1).wait_recv()
            relay_copy(1, mine).start()
            send_back(0)
        relay_copy(source, theirs).wait_recv()
        meta_arrived(2 + source)
        gather(2 + source, 0)

        @pl.loop(0, units // NARROW)
        def _(i):
            up_tile(CAP, i)

        if source == 1:
            local_copy.wait_recv()

        @pl.loop(0, model // WIDE)
        def _(n):
            cols = pl.ds(pl.multiple_of(n * WIDE, WIDE), WIDE)
            product = jnp.dot(hidden[0:CAP, :], down_w[:, cols], preferred_element_type=F32)
            far_out[source, :, cols] = spread(0, product).astype(BF16)
            if source == 1:
                @pl.when((core == 0) & ((n == 0) | (n == 4)))
                def _():
                    finish(lax.div(n, 4))

        swap_copy(source, theirs).start()

    send_back(1)

    @pl.when(core == 0)
    def _():
        @pl.loop(2, steps)
        def _(q):
            finish(q)

    @pl.when(core == 1)
    def _():
        @pl.loop(0, steps)
        def _(q):
            finish(q)

    for sender in range(2):
        for q in range(steps):
            hand_copy(sender, q).wait()
    for source in range(2):
        for q in range(steps):
            back_copy(source, q).wait_send()
        swap_copy(source, theirs).wait_send()
        x_copy(source).wait_send()
        relay_copy(source, mine).wait_send()
    sib_copy(0, theirs).wait_send()
    sib_copy(1, mine).wait_send()
    for copy in meta_copies:
        copy.wait_send()
    local_copy.wait_send()


def two_chips(sections, tokens, norm_gain, expert_ids, gate_values, gate_weight, up_weight, down_weight):
    count, model = tokens.shape[1:]
    units = gate_weight.shape[2]
    half = count // 2
    steps = half // STEP
    rows = 2 * CAP
    dma = pltpu.SemaphoreType.DMA
    vmem = pl.BlockSpec(memory_space=pltpu.VMEM)
    hbm = pl.BlockSpec(memory_space=pl.ANY)
    handed = pl.pallas_call(
        functools.partial(kernel, sections),
        out_shape=jax.ShapeDtypeStruct((count, model), BF16),
        in_specs=[vmem, vmem, vmem, vmem, hbm, hbm, hbm],
        out_specs=hbm,
        scratch_shapes=[
            pltpu.VMEM((model, units), BF16),
            pltpu.VMEM((model, units), BF16),
            pltpu.VMEM((units, model), BF16),
            pltpu.VMEM((4, count, model), BF16),
            pltpu.VMEM((4, 8, count), F32),
            pltpu.VMEM((2, CAP, count), BF16),
            pltpu.VMEM((2, CAP, 128), F32),
            pltpu.VMEM((rows, model), BF16),
            pltpu.VMEM((rows, units), BF16),
            pltpu.VMEM((count, model), F32),
            pltpu.VMEM((count, model), BF16),
            pltpu.VMEM((count, model), BF16),
            pltpu.VMEM((2, count, model), BF16),
            pltpu.VMEM((2, half, model), BF16),
            pltpu.VMEM((count, model), BF16),
            dma((2 * UP_CHUNKS + model // WIDE,)),
            dma((3,)), dma((3,)),
            dma((2,)), dma((2,)),
            dma((2,)), dma((2,)),
            dma((2,)), dma((2,)),
            dma((1,)), dma((1,)),
            dma((2,)), dma((2,)),
            dma((2 * steps,)), dma((2 * steps,)),
            dma((2 * steps,)), dma((2 * steps,)),
        ],
        compiler_params=pltpu.CompilerParams(
            collective_id=0, has_side_effects=True, vmem_limit_bytes=VMEM_LIMIT
        ),
        cost_estimate=pl.CostEstimate(
            flops=6 * EXPERTS * CAP * model * units, bytes_accessed=6 * model * units,
            transcendentals=EXPERTS * CAP * units,
        ),
    )(
        tokens[0], norm_gain, expert_ids[0].T, gate_values[0].T,
        gate_weight[0], up_weight[0], down_weight[0],
    )
    return handed[None]


VMEM_LIMIT = 63 * 1024 * 1024


def shifted(shard, axis, by):
    devices = lax.axis_size(axis)
    return lax.ppermute(shard, axis, [(i, (i + by) % devices) for i in range(devices)])


def on_device(tokens, norm_gain, expert_ids, gate_values, gate_weight, up_weight, down_weight):
    resident = tokens[0]
    choice_ids = expert_ids[0]
    weights_in = gate_values[0]
    gate_local = gate_weight[0]
    up_local = up_weight[0]
    down_local = down_weight[0]
    owners = lax.axis_size("expert")
    shards = owners // EXPERTS
    tok_count = resident.shape[0]
    model_dim = resident.shape[1]
    capacity = CAP
    widened = resident.astype(jnp.float32)
    scale = lax.rsqrt(jnp.mean(widened * widened, axis=-1, keepdims=True) + 1e-06)
    normed = (widened * scale * norm_gain[0][None, :]).astype(jnp.bfloat16)
    flat_ids = choice_ids.reshape(-1)
    onehot = (flat_ids[:, None] == jnp.arange(EXPERTS, dtype=jnp.int32)[None, :]).astype(jnp.int32)
    position = jnp.cumsum(onehot, axis=0) - 1
    slot_of = jnp.sum(position * onehot, axis=1).reshape(tok_count, TOP)
    target = choice_ids * capacity + slot_of
    dispatch_matrix = jnp.sum(
        (
            target[:, :, None] == jnp.arange(EXPERTS * capacity, dtype=jnp.int32)[None, None, :]
        ).astype(jnp.bfloat16),
        axis=1,
    )
    outgoing = jnp.einsum(
        "tr,td->rd", dispatch_matrix, normed, preferred_element_type=jnp.float32
    ).astype(jnp.bfloat16)
    outgoing = jnp.repeat(outgoing.reshape(EXPERTS, capacity, model_dim), shards, axis=0)
    arrived = lax.all_to_all(outgoing, "expert", split_axis=0, concat_axis=0, tiled=True)
    sources = arrived.shape[0]
    count = arrived.shape[1]
    flat_rows = arrived.reshape(sources * count, model_dim)
    gate = jnp.dot(flat_rows, gate_local, preferred_element_type=jnp.float32)
    upward = jnp.dot(flat_rows, up_local, preferred_element_type=jnp.float32)
    hidden = (jax.nn.silu(gate) * upward).astype(jnp.bfloat16)
    partial_out = jnp.dot(hidden, down_local, preferred_element_type=jnp.float32).astype(
        jnp.bfloat16
    )
    partials = partial_out.reshape(sources, count, model_dim)
    returned = lax.all_to_all(partials, "expert", split_axis=0, concat_axis=0, tiled=True)
    summed = jnp.sum(
        returned.astype(jnp.float32).reshape(EXPERTS, shards, capacity, model_dim), axis=1
    )
    picked = summed.reshape(EXPERTS * capacity, model_dim)[target]
    mixture = jnp.sum(weights_in[:, :, None] * picked, axis=1)
    layer_out = (widened + mixture).astype(jnp.bfloat16)
    handed = shifted(layer_out, "section", 1)
    return handed[None]


def solution(mesh):
    in_specs = (
        P("section", "expert", None),
        P("section", None),
        P("section", "expert", None),
        P("section", "expert", None),
        P("section", None, "expert"),
        P("section", None, "expert"),
        P("section", "expert", None),
    )
    out_specs = P("section", "expert", None)
    if mesh.shape["expert"] == EXPERTS:
        on_one = functools.partial(two_chips, mesh.shape["section"])
    else:
        on_one = on_device
    return jax.shard_map(
        on_one, mesh=mesh, in_specs=in_specs, out_specs=out_specs, check_vma=False
    )
```

```python
import functools

import jax
import jax.numpy as jnp
from jax import lax
from jax.experimental import pallas as pl
from jax.experimental.pallas import tpu as pltpu
from jax.sharding import PartitionSpec as P

EXPERTS = 4
TOP = 2
CAP = 80
MESH = pl.DeviceIdType.MESH
F32 = jnp.float32
BF16 = jnp.bfloat16
UP_CHUNKS = 4
WIDE = 512
NARROW = 256
STEP = 16
COPIES = 8


def kernel(
    sections, tok, gain, ids, gates, gate_hbm, up_hbm, down_hbm, out,
    gate_w, up_w, down_w, nrm, meta, pick, scale, rows_in, hidden, base, local_out, local_in,
    far_out, far_in, back,
    w_sem, meta_s, meta_r, sib_s, sib_r, x_s, x_r, relay_s, relay_r, local_s, local_r,
    swap_s, swap_r, back_s, back_r, hand_s, hand_r,
):
    tokens, model = tok.shape
    units = gate_w.shape[1]
    half = tokens // 2
    tiles = model // WIDE
    section = lax.axis_index("section")
    me = lax.axis_index("expert")
    chip = lax.div(me, 2)
    core = lax.rem(me, 2)
    other = 1 - core
    sibling = chip * 2 + other
    far_chip = (1 - chip) * 2
    after = lax.rem(section + 1, sections)
    before = lax.rem(section + sections - 1, sections)
    mine = pl.ds(pl.multiple_of(core * half, half), half)
    theirs = pl.ds(pl.multiple_of(other * half, half), half)

    def remote(src, dst, send, recv, **device):
        return pltpu.make_async_remote_copy(
            src_ref=src, dst_ref=dst, send_sem=send, recv_sem=recv,
            device_id=device, device_id_type=MESH,
        )

    barrier = pltpu.get_barrier_semaphore()
    for peer in (sibling, far_chip, far_chip + 1):
        pl.semaphore_signal(barrier, inc=1, device_id={"expert": peer}, device_id_type=MESH)
    for peer in (after, before):
        pl.semaphore_signal(barrier, inc=1, device_id={"section": peer}, device_id_type=MESH)

    up_width = units // UP_CHUNKS

    def gate_copy(k):
        cols = pl.ds(pl.multiple_of(k * up_width, up_width), up_width)
        return pltpu.make_async_copy(gate_hbm.at[:, cols], gate_w.at[:, cols], w_sem.at[k])

    def up_copy(k):
        cols = pl.ds(pl.multiple_of(k * up_width, up_width), up_width)
        return pltpu.make_async_copy(up_hbm.at[:, cols], up_w.at[:, cols], w_sem.at[UP_CHUNKS + k])

    def down_copy(k):
        cols = pl.ds(pl.multiple_of(k * WIDE, WIDE), WIDE)
        return pltpu.make_async_copy(
            down_hbm.at[:, cols], down_w.at[:, cols], w_sem.at[2 * UP_CHUNKS + k]
        )

    for k in range(UP_CHUNKS):
        gate_copy(k).start()
        up_copy(k).start()
    for k in range(model // WIDE):
        down_copy(k).start()

    meta[0] = jnp.zeros(meta.shape[1:], F32)
    meta[0, 0:TOP, :] = ids[...].astype(F32)
    meta[0, TOP:2 * TOP, :] = gates[...]

    @pl.loop(0, tokens // STEP)
    def _(i):
        rows = pl.ds(pl.multiple_of(i * STEP, STEP), STEP)
        widened = tok[rows, :].astype(F32)
        inverse = lax.rsqrt(jnp.mean(widened * widened, axis=-1, keepdims=True) + 1e-06)
        nrm[0, rows, :] = (widened * inverse * gain[...]).astype(BF16)

    pl.semaphore_wait(barrier, 5)

    def sib_copy(k, rows):
        return remote(
            nrm.at[0, rows], nrm.at[1, rows], sib_s.at[k], sib_r.at[k], expert=sibling
        )

    def x_copy(source):
        slot = lax.rem(source + 2 - core, 2)
        return remote(
            nrm.at[slot, mine], nrm.at[2 + source, mine], x_s.at[source], x_r.at[source],
            expert=far_chip + core,
        )

    def relay_copy(source, rows):
        return remote(
            nrm.at[2 + source, rows], nrm.at[2 + source, rows], relay_s.at[source],
            relay_r.at[source], expert=sibling,
        )

    meta_copies = [
        remote(meta.at[0], meta.at[1], meta_s.at[0], meta_r.at[0], expert=sibling),
        remote(meta.at[0], meta.at[2 + core], meta_s.at[1], meta_r.at[1 + core], expert=far_chip),
        remote(
            meta.at[0], meta.at[2 + core], meta_s.at[2], meta_r.at[1 + core], expert=far_chip + 1
        ),
    ]
    sib_copy(0, theirs).start()

    @pl.when(core == 0)
    def _():
        x_copy(0).start()

    for copy in meta_copies:
        copy.start()
    sib_copy(1, mine).start()
    sib_copy(0, mine).wait_recv()

    @pl.when(core == 1)
    def _():
        x_copy(0).start()

    x_copy(1).start()

    def meta_arrived(slot):
        remote(
            meta.at[0], meta.at[slot], meta_s.at[0], meta_r.at[slot - 1], expert=sibling
        ).wait_recv()

    def gather(slot, place):
        expert = me.astype(F32)
        about = meta[slot]
        first = about[0:1, :] == expert
        second = about[1:2, :] == expert
        chosen = jnp.where(first, 1.0, 0.0) + jnp.where(second, 1.0, 0.0)
        weight = jnp.where(first, about[2:3, :], 0.0) + jnp.where(second, about[3:4, :], 0.0)
        upper = jnp.where(
            lax.broadcasted_iota(jnp.int32, (tokens, tokens), 0)
            < lax.broadcasted_iota(jnp.int32, (tokens, tokens), 1),
            1.0, 0.0,
        ).astype(BF16)
        ahead = jnp.dot(
            jnp.broadcast_to(chosen, (16, tokens)).astype(BF16), upper,
            preferred_element_type=F32,
        )[0:1, :]
        wanted = lax.broadcasted_iota(jnp.int32, (CAP, tokens), 0).astype(F32)
        picked = jnp.where(ahead == wanted, 1.0, 0.0) * chosen
        pick[place] = picked.astype(BF16)
        scale[place] = jnp.broadcast_to(
            jnp.sum(picked * weight, axis=1, keepdims=True), (CAP, scale.shape[2])
        )

        @pl.loop(0, model // WIDE)
        def _(n):
            cols = pl.ds(pl.multiple_of(n * WIDE, WIDE), WIDE)
            rows_in[place * CAP:(place + 1) * CAP, cols] = jnp.dot(
                pick[place], nrm[slot, :, cols], preferred_element_type=F32
            ).astype(BF16)

    def up_tile(count, i):
        cols = pl.ds(pl.multiple_of(i * NARROW, NARROW), NARROW)
        gate = jnp.dot(rows_in[0:count, :], gate_w[:, cols], preferred_element_type=F32)
        upward = jnp.dot(rows_in[0:count, :], up_w[:, cols], preferred_element_type=F32)
        hidden[0:count, cols] = (jax.nn.silu(gate) * upward).astype(BF16)

    def spread(place, product):
        weighted = (
            product[place * CAP:(place + 1) * CAP, :] * scale[place][:, 0:1]
        ).astype(BF16)
        return lax.dot_general(
            pick[place], weighted, (((0,), (0,)), ((), ())), preferred_element_type=F32
        )

    def wide(n):
        return pl.ds(pl.multiple_of(n * WIDE, WIDE), WIDE)

    def local_copy(n):
        return remote(
            local_out.at[:, wide(n)], local_in.at[:, wide(n)], local_s.at[n], local_r.at[n],
            expert=sibling,
        )

    def swap_copy(source, n):
        return remote(
            far_out.at[source, theirs, wide(n)], far_in.at[source, :, wide(n)],
            swap_s.at[source * tiles + n], swap_r.at[source * tiles + n], expert=sibling,
        )

    def back_copy(source, n):
        return remote(
            far_out.at[source, mine, wide(n)], back.at[mine, wide(n)],
            back_s.at[source * tiles + n], back_r.at[core * tiles + n],
            expert=far_chip + source,
        )

    def hand_copy(n):
        return remote(
            back.at[:, wide(n)], out.at[:, wide(n)], hand_s.at[n], hand_r.at[n], section=after
        )

    def settle(source, n):
        swap_copy(source, n).wait_recv()
        far_out[source, mine, wide(n)] = (
            far_out[source, mine, wide(n)].astype(F32) + far_in[source, :, wide(n)].astype(F32)
        ).astype(BF16)
        back_copy(source, n).start()

    def finish(n):
        local_copy(n).wait_recv()
        for sender in range(2):
            rows = pl.ds(sender * half, half)
            remote(
                back.at[rows, wide(n)], back.at[rows, wide(n)], back_s.at[0],
                back_r.at[sender * tiles + n], expert=far_chip,
            ).wait_recv()
        for first in range(0, tokens, 32):
            rows = pl.ds(first, 32)
            back[rows, wide(n)] = (
                base[rows, wide(n)] + local_in[rows, wide(n)].astype(F32)
                + back[rows, wide(n)].astype(F32)
            ).astype(BF16)
        hand_copy(n).start()

    def down_pass(source, place, extra):
        @pl.loop(0, tiles)
        def _(n):
            if source == 0:
                down_copy(n).wait()
            for part in range(WIDE // NARROW):
                cols = pl.ds(pl.multiple_of(n * WIDE + part * NARROW, NARROW), NARROW)
                product = jnp.dot(
                    hidden[0:(place + 1) * CAP, :], down_w[:, cols], preferred_element_type=F32
                )
                far_out[source, :, cols] = spread(place, product).astype(BF16)
                if source == 0:
                    base[:, cols] = tok[:, cols].astype(F32) + spread(0, product)
                    local_out[:, cols] = spread(1, product).astype(BF16)
            swap_copy(source, n).start()
            if source == 0:
                local_copy(n).start()

            @pl.when(n > 0)
            def _():
                settle(source, n - 1)

            extra(n)

        settle(source, tiles - 1)

    gather(0, 0)
    sib_copy(1, theirs).wait_recv()
    meta_arrived(1)
    gather(1, 1)
    x_copy(0).wait_recv()
    relay_copy(0, mine).start()
    meta_arrived(2)
    relay_copy(0, theirs).wait_recv()
    gather(2, 2)

    @pl.loop(0, UP_CHUNKS)
    def _(k):
        gate_copy(k).wait()
        up_copy(k).wait()

        @pl.loop(0, up_width // NARROW)
        def _(i):
            up_tile(3 * CAP, k * (up_width // NARROW) + i)

    def relay_next(n):
        @pl.when(n == tiles - 2)
        def _():
            x_copy(1).wait_recv()
            relay_copy(1, mine).start()

    down_pass(0, 2, relay_next)

    meta_arrived(3)
    relay_copy(1, theirs).wait_recv()
    gather(3, 0)
    early = units // NARROW // 2 - 1

    @pl.loop(0, units // NARROW)
    def _(i):
        up_tile(CAP, i)

        @pl.when((core == 0) & (i >= 2) & (lax.rem(i, 2) == 0))
        def _():
            finish(lax.div(i, 2) - 1)

    def hand_early(n):
        @pl.when((core == 0) & (n < 5) & (lax.rem(n, 2) == 0))
        def _():
            finish(early + lax.div(n, 2))

    down_pass(1, 0, hand_early)

    @pl.when(core == 0)
    def _():
        @pl.loop(early + 3, tiles)
        def _(n):
            finish(n)

    @pl.when(core == 1)
    def _():
        @pl.loop(0, tiles)
        def _(n):
            finish(n)

    @pl.loop(0, tiles)
    def _(n):
        hand_copy(n).wait()
        local_copy(n).wait_send()
        for source in range(2):
            back_copy(source, n).wait_send()
            swap_copy(source, n).wait_send()

    for source in range(2):
        x_copy(source).wait_send()
        relay_copy(source, mine).wait_send()
    sib_copy(0, theirs).wait_send()
    sib_copy(1, mine).wait_send()
    for copy in meta_copies:
        copy.wait_send()


def copy_out(src, dst, sem):
    rows = src.shape[0] // COPIES
    copies = [
        pltpu.make_async_copy(
            src.at[pl.ds(k * rows, rows)], dst.at[pl.ds(k * rows, rows)], sem.at[k]
        )
        for k in range(COPIES)
    ]
    for copy in copies:
        copy.start()
    for copy in copies:
        copy.wait()


def two_chips(sections, tokens, norm_gain, expert_ids, gate_values, gate_weight, up_weight, down_weight):
    count, model = tokens.shape[1:]
    units = gate_weight.shape[2]
    half = count // 2
    tiles = model // WIDE
    rows = 3 * CAP
    dma = pltpu.SemaphoreType.DMA
    vmem = pl.BlockSpec(memory_space=pltpu.VMEM)
    hbm = pl.BlockSpec(memory_space=pl.ANY)
    handed = pl.pallas_call(
        functools.partial(kernel, sections),
        out_shape=jax.ShapeDtypeStruct((count, model), BF16),
        in_specs=[vmem, vmem, vmem, vmem, hbm, hbm, hbm],
        out_specs=hbm,
        scratch_shapes=[
            pltpu.VMEM((model, units), BF16),
            pltpu.VMEM((model, units), BF16),
            pltpu.VMEM((units, model), BF16),
            pltpu.VMEM((4, count, model), BF16),
            pltpu.VMEM((4, 8, count), F32),
            pltpu.VMEM((3, CAP, count), BF16),
            pltpu.VMEM((3, CAP, 128), F32),
            pltpu.VMEM((rows, model), BF16),
            pltpu.VMEM((rows, units), BF16),
            pltpu.VMEM((count, model), F32),
            pltpu.VMEM((count, model), BF16),
            pltpu.VMEM((count, model), BF16),
            pltpu.VMEM((2, count, model), BF16),
            pltpu.VMEM((2, half, model), BF16),
            pltpu.VMEM((count, model), BF16),
            dma((2 * UP_CHUNKS + model // WIDE,)),
            dma((3,)), dma((3,)),
            dma((2,)), dma((2,)),
            dma((2,)), dma((2,)),
            dma((2,)), dma((2,)),
            dma((tiles,)), dma((tiles,)),
            dma((2 * tiles,)), dma((2 * tiles,)),
            dma((2 * tiles,)), dma((2 * tiles,)),
            dma((tiles,)), dma((tiles,)),
        ],
        compiler_params=pltpu.CompilerParams(
            collective_id=0, has_side_effects=True, vmem_limit_bytes=VMEM_LIMIT
        ),
        cost_estimate=pl.CostEstimate(
            flops=6 * EXPERTS * CAP * model * units, bytes_accessed=6 * model * units,
            transcendentals=EXPERTS * CAP * units,
        ),
    )(
        tokens[0], norm_gain, expert_ids[0].T, gate_values[0].T,
        gate_weight[0], up_weight[0], down_weight[0],
    )
    copied = pl.pallas_call(
        copy_out,
        out_shape=jax.ShapeDtypeStruct((count, model), BF16),
        in_specs=[hbm],
        out_specs=hbm,
        scratch_shapes=[dma((COPIES,))],
        compiler_params=pltpu.CompilerParams(vmem_limit_bytes=VMEM_LIMIT),
        cost_estimate=pl.CostEstimate(
            flops=0, bytes_accessed=4 * count * model, transcendentals=0
        ),
    )(handed)
    return copied[None]


VMEM_LIMIT = 63 * 1024 * 1024


def shifted(shard, axis, by):
    devices = lax.axis_size(axis)
    return lax.ppermute(shard, axis, [(i, (i + by) % devices) for i in range(devices)])


def on_device(tokens, norm_gain, expert_ids, gate_values, gate_weight, up_weight, down_weight):
    resident = tokens[0]
    choice_ids = expert_ids[0]
    weights_in = gate_values[0]
    gate_local = gate_weight[0]
    up_local = up_weight[0]
    down_local = down_weight[0]
    owners = lax.axis_size("expert")
    shards = owners // EXPERTS
    tok_count = resident.shape[0]
    model_dim = resident.shape[1]
    capacity = CAP
    widened = resident.astype(jnp.float32)
    scale = lax.rsqrt(jnp.mean(widened * widened, axis=-1, keepdims=True) + 1e-06)
    normed = (widened * scale * norm_gain[0][None, :]).astype(jnp.bfloat16)
    flat_ids = choice_ids.reshape(-1)
    onehot = (flat_ids[:, None] == jnp.arange(EXPERTS, dtype=jnp.int32)[None, :]).astype(jnp.int32)
    position = jnp.cumsum(onehot, axis=0) - 1
    slot_of = jnp.sum(position * onehot, axis=1).reshape(tok_count, TOP)
    target = choice_ids * capacity + slot_of
    dispatch_matrix = jnp.sum(
        (
            target[:, :, None] == jnp.arange(EXPERTS * capacity, dtype=jnp.int32)[None, None, :]
        ).astype(jnp.bfloat16),
        axis=1,
    )
    outgoing = jnp.einsum(
        "tr,td->rd", dispatch_matrix, normed, preferred_element_type=jnp.float32
    ).astype(jnp.bfloat16)
    outgoing = jnp.repeat(outgoing.reshape(EXPERTS, capacity, model_dim), shards, axis=0)
    arrived = lax.all_to_all(outgoing, "expert", split_axis=0, concat_axis=0, tiled=True)
    sources = arrived.shape[0]
    count = arrived.shape[1]
    flat_rows = arrived.reshape(sources * count, model_dim)
    gate = jnp.dot(flat_rows, gate_local, preferred_element_type=jnp.float32)
    upward = jnp.dot(flat_rows, up_local, preferred_element_type=jnp.float32)
    hidden = (jax.nn.silu(gate) * upward).astype(jnp.bfloat16)
    partial_out = jnp.dot(hidden, down_local, preferred_element_type=jnp.float32).astype(
        jnp.bfloat16
    )
    partials = partial_out.reshape(sources, count, model_dim)
    returned = lax.all_to_all(partials, "expert", split_axis=0, concat_axis=0, tiled=True)
    summed = jnp.sum(
        returned.astype(jnp.float32).reshape(EXPERTS, shards, capacity, model_dim), axis=1
    )
    picked = summed.reshape(EXPERTS * capacity, model_dim)[target]
    mixture = jnp.sum(weights_in[:, :, None] * picked, axis=1)
    layer_out = (widened + mixture).astype(jnp.bfloat16)
    handed = shifted(layer_out, "section", 1)
    return handed[None]


def solution(mesh):
    in_specs = (
        P("section", "expert", None),
        P("section", None),
        P("section", "expert", None),
        P("section", "expert", None),
        P("section", None, "expert"),
        P("section", None, "expert"),
        P("section", "expert", None),
    )
    out_specs = P("section", "expert", None)
    if mesh.shape["expert"] == EXPERTS:
        on_one = functools.partial(two_chips, mesh.shape["section"])
    else:
        on_one = on_device
    return jax.shard_map(
        on_one, mesh=mesh, in_specs=in_specs, out_specs=out_specs, check_vma=False
    )
```

```python
import functools

import jax
import jax.numpy as jnp
from jax import lax
from jax.experimental import pallas as pl
from jax.experimental.pallas import tpu as pltpu
from jax.sharding import PartitionSpec as P

EXPERTS = 4
TOP = 2
CAP = 80
MESH = pl.DeviceIdType.MESH
F32 = jnp.float32
BF16 = jnp.bfloat16
UP_CHUNKS = 4
WIDE = 512
NARROW = 256
STEP = 16
COPIES = 4


def kernel(
    sections, tok, gain, ids, gates, gate_hbm, up_hbm, down_hbm, out,
    gate_w, up_w, down_w, nrm, meta, pick, put, scale, rows_in, hidden, base, local_out, local_in,
    far_out, far_in, back,
    w_sem, meta_s, meta_r, sib_s, sib_r, x_s, x_r, relay_s, relay_r, local_s, local_r,
    swap_s, swap_r, back_s, back_r, hand_s, hand_r,
):
    tokens, model = tok.shape
    units = gate_w.shape[1]
    half = tokens // 2
    tiles = model // WIDE
    section = lax.axis_index("section")
    me = lax.axis_index("expert")
    chip = lax.div(me, 2)
    core = lax.rem(me, 2)
    other = 1 - core
    sibling = chip * 2 + other
    far_chip = (1 - chip) * 2
    after = lax.rem(section + 1, sections)
    before = lax.rem(section + sections - 1, sections)
    mine = pl.ds(pl.multiple_of(core * half, half), half)
    theirs = pl.ds(pl.multiple_of(other * half, half), half)

    def remote(src, dst, send, recv, **device):
        return pltpu.make_async_remote_copy(
            src_ref=src, dst_ref=dst, send_sem=send, recv_sem=recv,
            device_id=device, device_id_type=MESH,
        )

    barrier = pltpu.get_barrier_semaphore()
    for peer in (sibling, far_chip, far_chip + 1):
        pl.semaphore_signal(barrier, inc=1, device_id={"expert": peer}, device_id_type=MESH)
    for peer in (after, before):
        pl.semaphore_signal(barrier, inc=1, device_id={"section": peer}, device_id_type=MESH)

    up_width = units // UP_CHUNKS

    def gate_copy(k):
        cols = pl.ds(pl.multiple_of(k * up_width, up_width), up_width)
        return pltpu.make_async_copy(gate_hbm.at[:, cols], gate_w.at[:, cols], w_sem.at[k])

    def up_copy(k):
        cols = pl.ds(pl.multiple_of(k * up_width, up_width), up_width)
        return pltpu.make_async_copy(up_hbm.at[:, cols], up_w.at[:, cols], w_sem.at[UP_CHUNKS + k])

    def down_copy(k):
        cols = pl.ds(pl.multiple_of(k * WIDE, WIDE), WIDE)
        return pltpu.make_async_copy(
            down_hbm.at[:, cols], down_w.at[:, cols], w_sem.at[2 * UP_CHUNKS + k]
        )

    for k in range(2):
        gate_copy(k).start()
        up_copy(k).start()

    meta[0] = jnp.zeros(meta.shape[1:], F32)
    meta[0, 0:TOP, :] = ids[...].astype(F32)
    meta[0, TOP:2 * TOP, :] = gates[...]

    @pl.loop(0, tokens // STEP)
    def _(i):
        rows = pl.ds(pl.multiple_of(i * STEP, STEP), STEP)
        widened = tok[rows, :].astype(F32)
        inverse = lax.rsqrt(jnp.mean(widened * widened, axis=-1, keepdims=True) + 1e-06)
        nrm[0, rows, :] = (widened * inverse * gain[...]).astype(BF16)

    pl.semaphore_wait(barrier, 5)

    def sib_copy(k, rows):
        return remote(
            nrm.at[0, rows], nrm.at[1, rows], sib_s.at[k], sib_r.at[k], expert=sibling
        )

    def x_copy(source):
        slot = lax.rem(source + 2 - core, 2)
        return remote(
            nrm.at[slot, mine], nrm.at[2 + source, mine], x_s.at[source], x_r.at[source],
            expert=far_chip + core,
        )

    def relay_copy(source, rows):
        return remote(
            nrm.at[2 + source, rows], nrm.at[2 + source, rows], relay_s.at[source],
            relay_r.at[source], expert=sibling,
        )

    meta_copies = [
        remote(meta.at[0], meta.at[1], meta_s.at[0], meta_r.at[0], expert=sibling),
        remote(meta.at[0], meta.at[2 + core], meta_s.at[1], meta_r.at[1 + core], expert=far_chip),
        remote(
            meta.at[0], meta.at[2 + core], meta_s.at[2], meta_r.at[1 + core], expert=far_chip + 1
        ),
    ]
    sib_copy(0, theirs).start()

    @pl.when(core == 0)
    def _():
        x_copy(0).start()

    for copy in meta_copies:
        copy.start()
    sib_copy(1, mine).start()
    sib_copy(0, mine).wait_recv()

    @pl.when(core == 1)
    def _():
        x_copy(0).start()

    x_copy(1).start()
    gate_copy(2).start()
    up_copy(2).start()

    def meta_arrived(slot):
        remote(
            meta.at[0], meta.at[slot], meta_s.at[0], meta_r.at[slot - 1], expert=sibling
        ).wait_recv()

    def gather(slot, place):
        expert = me.astype(F32)
        about = meta[slot]
        first = about[0:1, :] == expert
        second = about[1:2, :] == expert
        chosen = jnp.where(first, 1.0, 0.0) + jnp.where(second, 1.0, 0.0)
        weight = jnp.where(first, about[2:3, :], 0.0) + jnp.where(second, about[3:4, :], 0.0)
        upper = jnp.where(
            lax.broadcasted_iota(jnp.int32, (tokens, tokens), 0)
            < lax.broadcasted_iota(jnp.int32, (tokens, tokens), 1),
            1.0, 0.0,
        ).astype(BF16)
        ahead = jnp.dot(
            jnp.broadcast_to(chosen, (16, tokens)).astype(BF16), upper,
            preferred_element_type=F32,
        )[0:1, :]
        wanted = lax.broadcasted_iota(jnp.int32, (CAP, tokens), 0).astype(F32)
        picked = jnp.where(ahead == wanted, 1.0, 0.0) * chosen
        pick[place] = picked.astype(BF16)
        put[place] = picked.T.astype(BF16)
        scale[place] = jnp.broadcast_to(
            jnp.sum(picked * weight, axis=1, keepdims=True), (CAP, scale.shape[2])
        )

        @pl.loop(0, model // WIDE)
        def _(n):
            cols = pl.ds(pl.multiple_of(n * WIDE, WIDE), WIDE)
            rows_in[place * CAP:(place + 1) * CAP, cols] = jnp.dot(
                pick[place], nrm[slot, :, cols], preferred_element_type=F32
            ).astype(BF16)

    def up_tile(count, i):
        cols = pl.ds(pl.multiple_of(i * NARROW, NARROW), NARROW)
        gate = jnp.dot(rows_in[0:count, :], gate_w[:, cols], preferred_element_type=F32)
        upward = jnp.dot(rows_in[0:count, :], up_w[:, cols], preferred_element_type=F32)
        hidden[0:count, cols] = (jax.nn.silu(gate) * upward).astype(BF16)

    def spread(place, product):
        weighted = (
            product[place * CAP:(place + 1) * CAP, :] * scale[place][:, 0:1]
        ).astype(BF16)
        return jnp.dot(put[place], weighted, preferred_element_type=F32)

    def wide(n):
        return pl.ds(pl.multiple_of(n * WIDE, WIDE), WIDE)

    def local_copy(n):
        return remote(
            local_out.at[:, wide(n)], local_in.at[:, wide(n)], local_s.at[n], local_r.at[n],
            expert=sibling,
        )

    def swap_copy(source, n):
        return remote(
            far_out.at[source, theirs, wide(n)], far_in.at[source, :, wide(n)],
            swap_s.at[source * tiles + n], swap_r.at[source * tiles + n], expert=sibling,
        )

    def back_copy(source, n):
        return remote(
            far_out.at[source, mine, wide(n)], back.at[mine, wide(n)],
            back_s.at[source * tiles + n], back_r.at[core * tiles + n],
            expert=far_chip + source,
        )

    def hand_copy(n):
        return remote(
            back.at[:, wide(n)], out.at[:, wide(n)], hand_s.at[n], hand_r.at[n], section=after
        )

    def settle(source, n):
        swap_copy(source, n).wait_recv()
        far_out[source, mine, wide(n)] = (
            far_out[source, mine, wide(n)].astype(F32) + far_in[source, :, wide(n)].astype(F32)
        ).astype(BF16)
        back_copy(source, n).start()

    def finish(n):
        local_copy(n).wait_recv()
        for sender in range(2):
            rows = pl.ds(sender * half, half)
            remote(
                back.at[rows, wide(n)], back.at[rows, wide(n)], back_s.at[0],
                back_r.at[sender * tiles + n], expert=far_chip,
            ).wait_recv()
        for first in range(0, tokens, 32):
            rows = pl.ds(first, 32)
            back[rows, wide(n)] = (
                base[rows, wide(n)] + local_in[rows, wide(n)].astype(F32)
                + back[rows, wide(n)].astype(F32)
            ).astype(BF16)
        hand_copy(n).start()

    def down_pass(source, extra):
        @pl.loop(0, tiles)
        def _(n):
            for part in range(WIDE // NARROW):
                cols = pl.ds(pl.multiple_of(n * WIDE + part * NARROW, NARROW), NARROW)
                product = jnp.dot(
                    hidden[0:CAP, :], down_w[:, cols], preferred_element_type=F32
                )
                far_out[source, :, cols] = spread(0, product).astype(BF16)
            swap_copy(source, n).start()

            @pl.when(n > 0)
            def _():
                settle(source, n - 1)

            extra(n)

        settle(source, tiles - 1)

    gather(0, 0)
    sib_copy(1, theirs).wait_recv()
    meta_arrived(1)
    gather(1, 1)

    @pl.loop(0, UP_CHUNKS)
    def _(k):
        gate_copy(k).wait()
        up_copy(k).wait()

        @pl.when(k + 3 < UP_CHUNKS)
        def _():
            gate_copy(k + 3).start()
            up_copy(k + 3).start()

        @pl.when(k + 3 >= UP_CHUNKS)
        def _():
            down_copy(2 * (k + 3 - UP_CHUNKS)).start()
            down_copy(2 * (k + 3 - UP_CHUNKS) + 1).start()

        @pl.loop(0, up_width // NARROW)
        def _(i):
            up_tile(2 * CAP, k * (up_width // NARROW) + i)

    @pl.loop(0, tiles)
    def _(n):
        down_copy(n).wait()

        @pl.when(n + 6 < tiles)
        def _():
            down_copy(n + 6).start()

        for part in range(WIDE // NARROW):
            cols = pl.ds(pl.multiple_of(n * WIDE + part * NARROW, NARROW), NARROW)
            product = jnp.dot(hidden[...], down_w[:, cols], preferred_element_type=F32)
            base[:, cols] = tok[:, cols].astype(F32) + spread(0, product)
            local_out[:, cols] = spread(1, product).astype(BF16)
        local_copy(n).start()

        @pl.when(n == 4)
        def _():
            x_copy(0).wait_recv()
            relay_copy(0, mine).start()

    meta_arrived(2)
    relay_copy(0, theirs).wait_recv()
    gather(2, 0)

    @pl.loop(0, units // NARROW)
    def _(i):
        up_tile(CAP, i)

    def relay_next(n):
        @pl.when(n == tiles - 2)
        def _():
            x_copy(1).wait_recv()
            relay_copy(1, mine).start()

    down_pass(0, relay_next)

    meta_arrived(3)
    relay_copy(1, theirs).wait_recv()
    gather(3, 0)
    early = units // NARROW // 2 - 1

    @pl.loop(0, units // NARROW)
    def _(i):
        up_tile(CAP, i)

        @pl.when((core == 0) & (i >= 2) & (lax.rem(i, 2) == 0))
        def _():
            finish(lax.div(i, 2) - 1)

    def hand_early(n):
        @pl.when((core == 0) & (n < 5) & (lax.rem(n, 2) == 0))
        def _():
            finish(early + lax.div(n, 2))

    down_pass(1, hand_early)

    @pl.when(core == 0)
    def _():
        @pl.loop(early + 3, tiles)
        def _(n):
            finish(n)

    @pl.when(core == 1)
    def _():
        @pl.loop(0, tiles)
        def _(n):
            finish(n)

    @pl.loop(0, tiles)
    def _(n):
        hand_copy(n).wait()
        local_copy(n).wait_send()
        for source in range(2):
            back_copy(source, n).wait_send()
            swap_copy(source, n).wait_send()

    for source in range(2):
        x_copy(source).wait_send()
        relay_copy(source, mine).wait_send()
    sib_copy(0, theirs).wait_send()
    sib_copy(1, mine).wait_send()
    for copy in meta_copies:
        copy.wait_send()


def copy_out(src, dst, held, in_sem, out_sem):
    rows = src.shape[0] // COPIES
    ins, outs = [], []
    for k in range(COPIES):
        part = pl.ds(k * rows, rows)
        ins.append(pltpu.make_async_copy(src.at[part], held.at[part], in_sem.at[k]))
        outs.append(pltpu.make_async_copy(held.at[part], dst.at[part], out_sem.at[k]))
    for copy in ins:
        copy.start()
    for k in range(COPIES):
        ins[k].wait()
        outs[k].start()
    for copy in outs:
        copy.wait()


def two_chips(sections, tokens, norm_gain, expert_ids, gate_values, gate_weight, up_weight, down_weight):
    count, model = tokens.shape[1:]
    units = gate_weight.shape[2]
    half = count // 2
    tiles = model // WIDE
    rows = 2 * CAP
    dma = pltpu.SemaphoreType.DMA
    vmem = pl.BlockSpec(memory_space=pltpu.VMEM)
    hbm = pl.BlockSpec(memory_space=pl.ANY)
    handed = pl.pallas_call(
        functools.partial(kernel, sections),
        out_shape=jax.ShapeDtypeStruct((count, model), BF16),
        in_specs=[vmem, vmem, vmem, vmem, hbm, hbm, hbm],
        out_specs=hbm,
        scratch_shapes=[
            pltpu.VMEM((model, units), BF16),
            pltpu.VMEM((model, units), BF16),
            pltpu.VMEM((units, model), BF16),
            pltpu.VMEM((4, count, model), BF16),
            pltpu.VMEM((4, 8, count), F32),
            pltpu.VMEM((2, CAP, count), BF16),
            pltpu.VMEM((2, count, CAP), BF16),
            pltpu.VMEM((2, CAP, 128), F32),
            pltpu.VMEM((rows, model), BF16),
            pltpu.VMEM((rows, units), BF16),
            pltpu.VMEM((count, model), F32),
            pltpu.VMEM((count, model), BF16),
            pltpu.VMEM((count, model), BF16),
            pltpu.VMEM((2, count, model), BF16),
            pltpu.VMEM((2, half, model), BF16),
            pltpu.VMEM((count, model), BF16),
            dma((2 * UP_CHUNKS + model // WIDE,)),
            dma((3,)), dma((3,)),
            dma((2,)), dma((2,)),
            dma((2,)), dma((2,)),
            dma((2,)), dma((2,)),
            dma((tiles,)), dma((tiles,)),
            dma((2 * tiles,)), dma((2 * tiles,)),
            dma((2 * tiles,)), dma((2 * tiles,)),
            dma((tiles,)), dma((tiles,)),
        ],
        compiler_params=pltpu.CompilerParams(
            collective_id=0, has_side_effects=True, vmem_limit_bytes=VMEM_LIMIT
        ),
        cost_estimate=pl.CostEstimate(
            flops=6 * EXPERTS * CAP * model * units, bytes_accessed=6 * model * units,
            transcendentals=EXPERTS * CAP * units,
        ),
    )(
        tokens[0], norm_gain, expert_ids[0].T, gate_values[0].T,
        gate_weight[0], up_weight[0], down_weight[0],
    )
    copied = pl.pallas_call(
        copy_out,
        out_shape=jax.ShapeDtypeStruct((count, model), BF16),
        in_specs=[hbm],
        out_specs=hbm,
        scratch_shapes=[pltpu.VMEM((count, model), BF16), dma((COPIES,)), dma((COPIES,))],
        compiler_params=pltpu.CompilerParams(vmem_limit_bytes=VMEM_LIMIT),
        cost_estimate=pl.CostEstimate(
            flops=0, bytes_accessed=4 * count * model, transcendentals=0
        ),
    )(handed)
    return copied[None]


VMEM_LIMIT = 63 * 1024 * 1024


def shifted(shard, axis, by):
    devices = lax.axis_size(axis)
    return lax.ppermute(shard, axis, [(i, (i + by) % devices) for i in range(devices)])


def on_device(tokens, norm_gain, expert_ids, gate_values, gate_weight, up_weight, down_weight):
    resident = tokens[0]
    choice_ids = expert_ids[0]
    weights_in = gate_values[0]
    gate_local = gate_weight[0]
    up_local = up_weight[0]
    down_local = down_weight[0]
    owners = lax.axis_size("expert")
    shards = owners // EXPERTS
    tok_count = resident.shape[0]
    model_dim = resident.shape[1]
    capacity = CAP
    widened = resident.astype(jnp.float32)
    scale = lax.rsqrt(jnp.mean(widened * widened, axis=-1, keepdims=True) + 1e-06)
    normed = (widened * scale * norm_gain[0][None, :]).astype(jnp.bfloat16)
    flat_ids = choice_ids.reshape(-1)
    onehot = (flat_ids[:, None] == jnp.arange(EXPERTS, dtype=jnp.int32)[None, :]).astype(jnp.int32)
    position = jnp.cumsum(onehot, axis=0) - 1
    slot_of = jnp.sum(position * onehot, axis=1).reshape(tok_count, TOP)
    target = choice_ids * capacity + slot_of
    dispatch_matrix = jnp.sum(
        (
            target[:, :, None] == jnp.arange(EXPERTS * capacity, dtype=jnp.int32)[None, None, :]
        ).astype(jnp.bfloat16),
        axis=1,
    )
    outgoing = jnp.einsum(
        "tr,td->rd", dispatch_matrix, normed, preferred_element_type=jnp.float32
    ).astype(jnp.bfloat16)
    outgoing = jnp.repeat(outgoing.reshape(EXPERTS, capacity, model_dim), shards, axis=0)
    arrived = lax.all_to_all(outgoing, "expert", split_axis=0, concat_axis=0, tiled=True)
    sources = arrived.shape[0]
    count = arrived.shape[1]
    flat_rows = arrived.reshape(sources * count, model_dim)
    gate = jnp.dot(flat_rows, gate_local, preferred_element_type=jnp.float32)
    upward = jnp.dot(flat_rows, up_local, preferred_element_type=jnp.float32)
    hidden = (jax.nn.silu(gate) * upward).astype(jnp.bfloat16)
    partial_out = jnp.dot(hidden, down_local, preferred_element_type=jnp.float32).astype(
        jnp.bfloat16
    )
    partials = partial_out.reshape(sources, count, model_dim)
    returned = lax.all_to_all(partials, "expert", split_axis=0, concat_axis=0, tiled=True)
    summed = jnp.sum(
        returned.astype(jnp.float32).reshape(EXPERTS, shards, capacity, model_dim), axis=1
    )
    picked = summed.reshape(EXPERTS * capacity, model_dim)[target]
    mixture = jnp.sum(weights_in[:, :, None] * picked, axis=1)
    layer_out = (widened + mixture).astype(jnp.bfloat16)
    handed = shifted(layer_out, "section", 1)
    return handed[None]


def solution(mesh):
    in_specs = (
        P("section", "expert", None),
        P("section", None),
        P("section", "expert", None),
        P("section", "expert", None),
        P("section", None, "expert"),
        P("section", None, "expert"),
        P("section", "expert", None),
    )
    out_specs = P("section", "expert", None)
    if mesh.shape["expert"] == EXPERTS:
        on_one = functools.partial(two_chips, mesh.shape["section"])
    else:
        on_one = on_device
    return jax.shard_map(
        on_one, mesh=mesh, in_specs=in_specs, out_specs=out_specs, check_vma=False
    )
```

```python
import functools

import jax
import jax.numpy as jnp
from jax import lax
from jax.experimental import pallas as pl
from jax.experimental.pallas import tpu as pltpu
from jax.sharding import PartitionSpec as P

EXPERTS = 4
TOP = 2
CAP = 80
MESH = pl.DeviceIdType.MESH
F32 = jnp.float32
BF16 = jnp.bfloat16
UP_CHUNKS = 4
WIDE = 512
NARROW = 256
STEP = 16


def kernel(
    sections, tok, gain, ids, gates, gate_hbm, up_hbm, down_hbm, out,
    gate_w, up_w, down_w, nrm, meta, pick, put, scale, rows_in, hidden, base, local_out, local_in,
    far_out, far_in, back,
    w_sem, meta_s, meta_r, sib_s, sib_r, x_s, x_r, relay_s, relay_r, local_s, local_r,
    swap_s, swap_r, back_s, back_r, hand_s, hand_r,
):
    tokens, model = tok.shape
    units = gate_w.shape[1]
    half = tokens // 2
    tiles = model // WIDE
    section = lax.axis_index("section")
    me = lax.axis_index("expert")
    chip = lax.div(me, 2)
    core = lax.rem(me, 2)
    other = 1 - core
    sibling = chip * 2 + other
    far_chip = (1 - chip) * 2
    after = lax.rem(section + 1, sections)
    before = lax.rem(section + sections - 1, sections)
    mine = pl.ds(pl.multiple_of(core * half, half), half)
    theirs = pl.ds(pl.multiple_of(other * half, half), half)

    def remote(src, dst, send, recv, **device):
        return pltpu.make_async_remote_copy(
            src_ref=src, dst_ref=dst, send_sem=send, recv_sem=recv,
            device_id=device, device_id_type=MESH,
        )

    barrier = pltpu.get_barrier_semaphore()
    for peer in (sibling, far_chip, far_chip + 1):
        pl.semaphore_signal(barrier, inc=1, device_id={"expert": peer}, device_id_type=MESH)
    for peer in (after, before):
        pl.semaphore_signal(barrier, inc=1, device_id={"section": peer}, device_id_type=MESH)

    up_width = units // UP_CHUNKS

    def gate_copy(k):
        cols = pl.ds(pl.multiple_of(k * up_width, up_width), up_width)
        return pltpu.make_async_copy(gate_hbm.at[:, cols], gate_w.at[:, cols], w_sem.at[k])

    def up_copy(k):
        cols = pl.ds(pl.multiple_of(k * up_width, up_width), up_width)
        return pltpu.make_async_copy(up_hbm.at[:, cols], up_w.at[:, cols], w_sem.at[UP_CHUNKS + k])

    def down_copy(k):
        cols = pl.ds(pl.multiple_of(k * WIDE, WIDE), WIDE)
        return pltpu.make_async_copy(
            down_hbm.at[:, cols], down_w.at[:, cols], w_sem.at[2 * UP_CHUNKS + k]
        )

    for k in range(2):
        gate_copy(k).start()
        up_copy(k).start()

    meta[0] = jnp.zeros(meta.shape[1:], F32)
    meta[0, 0:TOP, :] = ids[...].astype(F32)
    meta[0, TOP:2 * TOP, :] = gates[...]

    @pl.loop(0, tokens // STEP)
    def _(i):
        rows = pl.ds(pl.multiple_of(i * STEP, STEP), STEP)
        widened = tok[rows, :].astype(F32)
        inverse = lax.rsqrt(jnp.mean(widened * widened, axis=-1, keepdims=True) + 1e-06)
        nrm[0, rows, :] = (widened * inverse * gain[...]).astype(BF16)

    pl.semaphore_wait(barrier, 5)

    def sib_copy(k, rows):
        return remote(
            nrm.at[0, rows], nrm.at[1, rows], sib_s.at[k], sib_r.at[k], expert=sibling
        )

    def x_copy(source):
        slot = lax.rem(source + 2 - core, 2)
        return remote(
            nrm.at[slot, mine], nrm.at[2 + source, mine], x_s.at[source], x_r.at[source],
            expert=far_chip + core,
        )

    def relay_copy(source, rows):
        return remote(
            nrm.at[2 + source, rows], nrm.at[2 + source, rows], relay_s.at[source],
            relay_r.at[source], expert=sibling,
        )

    meta_copies = [
        remote(meta.at[0], meta.at[1], meta_s.at[0], meta_r.at[0], expert=sibling),
        remote(meta.at[0], meta.at[2 + core], meta_s.at[1], meta_r.at[1 + core], expert=far_chip),
        remote(
            meta.at[0], meta.at[2 + core], meta_s.at[2], meta_r.at[1 + core], expert=far_chip + 1
        ),
    ]
    sib_copy(0, theirs).start()

    @pl.when(core == 0)
    def _():
        x_copy(0).start()

    for copy in meta_copies:
        copy.start()
    sib_copy(1, mine).start()
    sib_copy(0, mine).wait_recv()

    @pl.when(core == 1)
    def _():
        x_copy(0).start()

    x_copy(1).start()
    gate_copy(2).start()
    up_copy(2).start()

    def meta_arrived(slot):
        remote(
            meta.at[0], meta.at[slot], meta_s.at[0], meta_r.at[slot - 1], expert=sibling
        ).wait_recv()

    def gather(slot, place):
        expert = me.astype(F32)
        about = meta[slot]
        first = about[0:1, :] == expert
        second = about[1:2, :] == expert
        chosen = jnp.where(first, 1.0, 0.0) + jnp.where(second, 1.0, 0.0)
        weight = jnp.where(first, about[2:3, :], 0.0) + jnp.where(second, about[3:4, :], 0.0)
        upper = jnp.where(
            lax.broadcasted_iota(jnp.int32, (tokens, tokens), 0)
            < lax.broadcasted_iota(jnp.int32, (tokens, tokens), 1),
            1.0, 0.0,
        ).astype(BF16)
        ahead = jnp.dot(
            jnp.broadcast_to(chosen, (16, tokens)).astype(BF16), upper,
            preferred_element_type=F32,
        )[0:1, :]
        wanted = lax.broadcasted_iota(jnp.int32, (CAP, tokens), 0).astype(F32)
        picked = jnp.where(ahead == wanted, 1.0, 0.0) * chosen
        pick[place] = picked.astype(BF16)
        put[place] = picked.T.astype(BF16)
        scale[place] = jnp.broadcast_to(
            jnp.sum(picked * weight, axis=1, keepdims=True), (CAP, scale.shape[2])
        )

        @pl.loop(0, model // WIDE)
        def _(n):
            cols = pl.ds(pl.multiple_of(n * WIDE, WIDE), WIDE)
            rows_in[place * CAP:(place + 1) * CAP, cols] = jnp.dot(
                pick[place], nrm[slot, :, cols], preferred_element_type=F32
            ).astype(BF16)

    def up_tile(count, i):
        cols = pl.ds(pl.multiple_of(i * NARROW, NARROW), NARROW)
        gate = jnp.dot(rows_in[0:count, :], gate_w[:, cols], preferred_element_type=F32)
        upward = jnp.dot(rows_in[0:count, :], up_w[:, cols], preferred_element_type=F32)
        hidden[0:count, cols] = (jax.nn.silu(gate) * upward).astype(BF16)

    def spread(place, product):
        weighted = (
            product[place * CAP:(place + 1) * CAP, :] * scale[place][:, 0:1]
        ).astype(BF16)
        return jnp.dot(put[place], weighted, preferred_element_type=F32)

    def local_copy(n):
        return remote(
            local_out.at[n], local_in.at[n], local_s.at[n], local_r.at[n],
            expert=sibling,
        )

    def swap_copy(source, n):
        return remote(
            far_out.at[source, n, theirs], far_in.at[source, n],
            swap_s.at[source * tiles + n], swap_r.at[source * tiles + n], expert=sibling,
        )

    def back_copy(source, n):
        return remote(
            far_out.at[source, n, mine], back.at[n, mine],
            back_s.at[source * tiles + n], back_r.at[core * tiles + n],
            expert=far_chip + source,
        )

    def hand_copy(n):
        return remote(
            back.at[n], out.at[n], hand_s.at[n], hand_r.at[n], section=after
        )

    def settle(source, n):
        swap_copy(source, n).wait_recv()
        far_out[source, n, mine, :] = (
            far_out[source, n, mine, :].astype(F32) + far_in[source, n].astype(F32)
        ).astype(BF16)
        back_copy(source, n).start()

    def finish(n):
        local_copy(n).wait_recv()
        for sender in range(2):
            rows = pl.ds(sender * half, half)
            remote(
                back.at[n, rows], back.at[n, rows], back_s.at[0],
                back_r.at[sender * tiles + n], expert=far_chip,
            ).wait_recv()
        for first in range(0, tokens, 32):
            rows = pl.ds(first, 32)
            back[n, rows, :] = (
                base[n, rows, :] + local_in[n, rows, :].astype(F32)
                + back[n, rows, :].astype(F32)
            ).astype(BF16)
        hand_copy(n).start()

    def down_pass(source, extra):
        @pl.loop(0, tiles)
        def _(n):
            for part in range(WIDE // NARROW):
                cols = pl.ds(pl.multiple_of(n * WIDE + part * NARROW, NARROW), NARROW)
                product = jnp.dot(
                    hidden[0:CAP, :], down_w[:, cols], preferred_element_type=F32
                )
                part_cols = pl.ds(part * NARROW, NARROW)
                far_out[source, n, :, part_cols] = spread(0, product).astype(BF16)
            swap_copy(source, n).start()

            @pl.when(n > 0)
            def _():
                settle(source, n - 1)

            extra(n)

        settle(source, tiles - 1)

    gather(0, 0)
    sib_copy(1, theirs).wait_recv()
    meta_arrived(1)
    gather(1, 1)

    @pl.loop(0, UP_CHUNKS)
    def _(k):
        gate_copy(k).wait()
        up_copy(k).wait()

        @pl.when(k + 3 < UP_CHUNKS)
        def _():
            gate_copy(k + 3).start()
            up_copy(k + 3).start()

        @pl.when(k + 3 >= UP_CHUNKS)
        def _():
            down_copy(2 * (k + 3 - UP_CHUNKS)).start()
            down_copy(2 * (k + 3 - UP_CHUNKS) + 1).start()

        @pl.loop(0, up_width // NARROW)
        def _(i):
            up_tile(2 * CAP, k * (up_width // NARROW) + i)

    @pl.loop(0, tiles)
    def _(n):
        down_copy(n).wait()

        @pl.when(n + 6 < tiles)
        def _():
            down_copy(n + 6).start()

        for part in range(WIDE // NARROW):
            cols = pl.ds(pl.multiple_of(n * WIDE + part * NARROW, NARROW), NARROW)
            product = jnp.dot(hidden[...], down_w[:, cols], preferred_element_type=F32)
            part_cols = pl.ds(part * NARROW, NARROW)
            base[n, :, part_cols] = tok[:, cols].astype(F32) + spread(0, product)
            local_out[n, :, part_cols] = spread(1, product).astype(BF16)
        local_copy(n).start()

        @pl.when(n == 4)
        def _():
            x_copy(0).wait_recv()
            relay_copy(0, mine).start()

    meta_arrived(2)
    relay_copy(0, theirs).wait_recv()
    gather(2, 0)

    @pl.loop(0, units // NARROW)
    def _(i):
        up_tile(CAP, i)

    def relay_next(n):
        @pl.when(n == tiles - 2)
        def _():
            x_copy(1).wait_recv()
            relay_copy(1, mine).start()

    down_pass(0, relay_next)

    meta_arrived(3)
    relay_copy(1, theirs).wait_recv()
    gather(3, 0)
    early = units // NARROW // 2 - 1

    @pl.loop(0, units // NARROW)
    def _(i):
        up_tile(CAP, i)

        @pl.when((core == 0) & (i >= 2) & (lax.rem(i, 2) == 0))
        def _():
            finish(lax.div(i, 2) - 1)

    def hand_early(n):
        @pl.when((core == 0) & (n < 5) & (lax.rem(n, 2) == 0))
        def _():
            finish(early + lax.div(n, 2))

    down_pass(1, hand_early)

    @pl.when(core == 0)
    def _():
        @pl.loop(early + 3, tiles)
        def _(n):
            finish(n)

    @pl.when(core == 1)
    def _():
        @pl.loop(0, tiles)
        def _(n):
            finish(n)

    @pl.loop(0, tiles)
    def _(n):
        hand_copy(n).wait()
        local_copy(n).wait_send()
        for source in range(2):
            back_copy(source, n).wait_send()
            swap_copy(source, n).wait_send()

    for source in range(2):
        x_copy(source).wait_send()
        relay_copy(source, mine).wait_send()
    sib_copy(0, theirs).wait_send()
    sib_copy(1, mine).wait_send()
    for copy in meta_copies:
        copy.wait_send()


def copy_out(src, dst, held, in_sem, out_sem):
    ins, outs = [], []
    for n in range(src.shape[0]):
        cols = pl.ds(n * WIDE, WIDE)
        ins.append(pltpu.make_async_copy(src.at[n], held.at[n], in_sem.at[n]))
        outs.append(pltpu.make_async_copy(held.at[n], dst.at[:, cols], out_sem.at[n]))
    for copy in ins:
        copy.start()
    for n in range(src.shape[0]):
        ins[n].wait()
        outs[n].start()
    for copy in outs:
        copy.wait()


def two_chips(sections, tokens, norm_gain, expert_ids, gate_values, gate_weight, up_weight, down_weight):
    count, model = tokens.shape[1:]
    units = gate_weight.shape[2]
    half = count // 2
    tiles = model // WIDE
    rows = 2 * CAP
    dma = pltpu.SemaphoreType.DMA
    vmem = pl.BlockSpec(memory_space=pltpu.VMEM)
    hbm = pl.BlockSpec(memory_space=pl.ANY)
    handed = pl.pallas_call(
        functools.partial(kernel, sections),
        out_shape=jax.ShapeDtypeStruct((tiles, count, WIDE), BF16),
        in_specs=[vmem, vmem, vmem, vmem, hbm, hbm, hbm],
        out_specs=hbm,
        scratch_shapes=[
            pltpu.VMEM((model, units), BF16),
            pltpu.VMEM((model, units), BF16),
            pltpu.VMEM((units, model), BF16),
            pltpu.VMEM((4, count, model), BF16),
            pltpu.VMEM((4, 8, count), F32),
            pltpu.VMEM((2, CAP, count), BF16),
            pltpu.VMEM((2, count, CAP), BF16),
            pltpu.VMEM((2, CAP, 128), F32),
            pltpu.VMEM((rows, model), BF16),
            pltpu.VMEM((rows, units), BF16),
            pltpu.VMEM((tiles, count, WIDE), F32),
            pltpu.VMEM((tiles, count, WIDE), BF16),
            pltpu.VMEM((tiles, count, WIDE), BF16),
            pltpu.VMEM((2, tiles, count, WIDE), BF16),
            pltpu.VMEM((2, tiles, half, WIDE), BF16),
            pltpu.VMEM((tiles, count, WIDE), BF16),
            dma((2 * UP_CHUNKS + model // WIDE,)),
            dma((3,)), dma((3,)),
            dma((2,)), dma((2,)),
            dma((2,)), dma((2,)),
            dma((2,)), dma((2,)),
            dma((tiles,)), dma((tiles,)),
            dma((2 * tiles,)), dma((2 * tiles,)),
            dma((2 * tiles,)), dma((2 * tiles,)),
            dma((tiles,)), dma((tiles,)),
        ],
        compiler_params=pltpu.CompilerParams(
            collective_id=0, has_side_effects=True, vmem_limit_bytes=VMEM_LIMIT
        ),
        cost_estimate=pl.CostEstimate(
            flops=6 * EXPERTS * CAP * model * units, bytes_accessed=6 * model * units,
            transcendentals=EXPERTS * CAP * units,
        ),
    )(
        tokens[0], norm_gain, expert_ids[0].T, gate_values[0].T,
        gate_weight[0], up_weight[0], down_weight[0],
    )
    copied = pl.pallas_call(
        copy_out,
        out_shape=jax.ShapeDtypeStruct((count, model), BF16),
        in_specs=[hbm],
        out_specs=hbm,
        scratch_shapes=[pltpu.VMEM((tiles, count, WIDE), BF16), dma((tiles,)), dma((tiles,))],
        compiler_params=pltpu.CompilerParams(vmem_limit_bytes=VMEM_LIMIT),
        cost_estimate=pl.CostEstimate(
            flops=0, bytes_accessed=4 * count * model, transcendentals=0
        ),
    )(handed)
    return copied[None]


VMEM_LIMIT = 63 * 1024 * 1024


def shifted(shard, axis, by):
    devices = lax.axis_size(axis)
    return lax.ppermute(shard, axis, [(i, (i + by) % devices) for i in range(devices)])


def on_device(tokens, norm_gain, expert_ids, gate_values, gate_weight, up_weight, down_weight):
    resident = tokens[0]
    choice_ids = expert_ids[0]
    weights_in = gate_values[0]
    gate_local = gate_weight[0]
    up_local = up_weight[0]
    down_local = down_weight[0]
    owners = lax.axis_size("expert")
    shards = owners // EXPERTS
    tok_count = resident.shape[0]
    model_dim = resident.shape[1]
    capacity = CAP
    widened = resident.astype(jnp.float32)
    scale = lax.rsqrt(jnp.mean(widened * widened, axis=-1, keepdims=True) + 1e-06)
    normed = (widened * scale * norm_gain[0][None, :]).astype(jnp.bfloat16)
    flat_ids = choice_ids.reshape(-1)
    onehot = (flat_ids[:, None] == jnp.arange(EXPERTS, dtype=jnp.int32)[None, :]).astype(jnp.int32)
    position = jnp.cumsum(onehot, axis=0) - 1
    slot_of = jnp.sum(position * onehot, axis=1).reshape(tok_count, TOP)
    target = choice_ids * capacity + slot_of
    dispatch_matrix = jnp.sum(
        (
            target[:, :, None] == jnp.arange(EXPERTS * capacity, dtype=jnp.int32)[None, None, :]
        ).astype(jnp.bfloat16),
        axis=1,
    )
    outgoing = jnp.einsum(
        "tr,td->rd", dispatch_matrix, normed, preferred_element_type=jnp.float32
    ).astype(jnp.bfloat16)
    outgoing = jnp.repeat(outgoing.reshape(EXPERTS, capacity, model_dim), shards, axis=0)
    arrived = lax.all_to_all(outgoing, "expert", split_axis=0, concat_axis=0, tiled=True)
    sources = arrived.shape[0]
    count = arrived.shape[1]
    flat_rows = arrived.reshape(sources * count, model_dim)
    gate = jnp.dot(flat_rows, gate_local, preferred_element_type=jnp.float32)
    upward = jnp.dot(flat_rows, up_local, preferred_element_type=jnp.float32)
    hidden = (jax.nn.silu(gate) * upward).astype(jnp.bfloat16)
    partial_out = jnp.dot(hidden, down_local, preferred_element_type=jnp.float32).astype(
        jnp.bfloat16
    )
    partials = partial_out.reshape(sources, count, model_dim)
    returned = lax.all_to_all(partials, "expert", split_axis=0, concat_axis=0, tiled=True)
    summed = jnp.sum(
        returned.astype(jnp.float32).reshape(EXPERTS, shards, capacity, model_dim), axis=1
    )
    picked = summed.reshape(EXPERTS * capacity, model_dim)[target]
    mixture = jnp.sum(weights_in[:, :, None] * picked, axis=1)
    layer_out = (widened + mixture).astype(jnp.bfloat16)
    handed = shifted(layer_out, "section", 1)
    return handed[None]


def solution(mesh):
    in_specs = (
        P("section", "expert", None),
        P("section", None),
        P("section", "expert", None),
        P("section", "expert", None),
        P("section", None, "expert"),
        P("section", None, "expert"),
        P("section", "expert", None),
    )
    out_specs = P("section", "expert", None)
    if mesh.shape["expert"] == EXPERTS:
        on_one = functools.partial(two_chips, mesh.shape["section"])
    else:
        on_one = on_device
    return jax.shard_map(
        on_one, mesh=mesh, in_specs=in_specs, out_specs=out_specs, check_vma=False
    )
```

```python
import functools

import jax
import jax.numpy as jnp
from jax import lax
from jax.experimental import pallas as pl
from jax.experimental.pallas import tpu as pltpu
from jax.sharding import PartitionSpec as P

EXPERTS = 4
TOP = 2
CAP = 80
MESH = pl.DeviceIdType.MESH
F32 = jnp.float32
BF16 = jnp.bfloat16
UP_CHUNKS = 4
WIDE = 512
NARROW = 256
STEP = 16
LAG = 3


def kernel(
    sections, tok, gain, ids, gates, gate_hbm, up_hbm, down_hbm, out,
    gate_w, up_w, down_w, nrm, meta, pick, put, scale, rows_in, hidden, base, local_out, local_in,
    far_out, far_in, back,
    w_sem, meta_s, meta_r, sib_s, sib_r, x_s, x_r, relay_s, relay_r, local_s, local_r,
    swap_s, swap_r, back_s, back_r, hand_s, hand_r,
):
    tokens, model = tok.shape
    units = gate_w.shape[1]
    half = tokens // 2
    tiles = model // WIDE
    section = lax.axis_index("section")
    me = lax.axis_index("expert")
    chip = lax.div(me, 2)
    core = lax.rem(me, 2)
    other = 1 - core
    sibling = chip * 2 + other
    far_chip = (1 - chip) * 2
    after = lax.rem(section + 1, sections)
    before = lax.rem(section + sections - 1, sections)
    mine = pl.ds(pl.multiple_of(core * half, half), half)
    theirs = pl.ds(pl.multiple_of(other * half, half), half)

    def remote(src, dst, send, recv, **device):
        return pltpu.make_async_remote_copy(
            src_ref=src, dst_ref=dst, send_sem=send, recv_sem=recv,
            device_id=device, device_id_type=MESH,
        )

    barrier = pltpu.get_barrier_semaphore()
    for peer in (sibling, far_chip, far_chip + 1):
        pl.semaphore_signal(barrier, inc=1, device_id={"expert": peer}, device_id_type=MESH)
    for peer in (after, before):
        pl.semaphore_signal(barrier, inc=1, device_id={"section": peer}, device_id_type=MESH)

    up_width = units // UP_CHUNKS

    def gate_copy(k):
        cols = pl.ds(pl.multiple_of(k * up_width, up_width), up_width)
        return pltpu.make_async_copy(gate_hbm.at[:, cols], gate_w.at[:, cols], w_sem.at[k])

    def up_copy(k):
        cols = pl.ds(pl.multiple_of(k * up_width, up_width), up_width)
        return pltpu.make_async_copy(up_hbm.at[:, cols], up_w.at[:, cols], w_sem.at[UP_CHUNKS + k])

    def down_copy(k):
        cols = pl.ds(pl.multiple_of(k * WIDE, WIDE), WIDE)
        return pltpu.make_async_copy(
            down_hbm.at[:, cols], down_w.at[:, cols], w_sem.at[2 * UP_CHUNKS + k]
        )

    for k in range(2):
        gate_copy(k).start()
        up_copy(k).start()

    meta[0] = jnp.zeros(meta.shape[1:], F32)
    meta[0, 0:TOP, :] = ids[...].astype(F32)
    meta[0, TOP:2 * TOP, :] = gates[...]

    @pl.loop(0, tokens // STEP)
    def _(i):
        rows = pl.ds(pl.multiple_of(i * STEP, STEP), STEP)
        widened = tok[rows, :].astype(F32)
        inverse = lax.rsqrt(jnp.mean(widened * widened, axis=-1, keepdims=True) + 1e-06)
        nrm[0, rows, :] = (widened * inverse * gain[...]).astype(BF16)

    pl.semaphore_wait(barrier, 5)

    def sib_copy(k, rows):
        return remote(
            nrm.at[0, rows], nrm.at[1, rows], sib_s.at[k], sib_r.at[k], expert=sibling
        )

    def x_copy(source):
        slot = lax.rem(source + 2 - core, 2)
        return remote(
            nrm.at[slot, mine], nrm.at[2 + source, mine], x_s.at[source], x_r.at[source],
            expert=far_chip + core,
        )

    def relay_copy(source, rows):
        return remote(
            nrm.at[2 + source, rows], nrm.at[2 + source, rows], relay_s.at[source],
            relay_r.at[source], expert=sibling,
        )

    meta_copies = [
        remote(meta.at[0], meta.at[1], meta_s.at[0], meta_r.at[0], expert=sibling),
        remote(meta.at[0], meta.at[2 + core], meta_s.at[1], meta_r.at[1 + core], expert=far_chip),
        remote(
            meta.at[0], meta.at[2 + core], meta_s.at[2], meta_r.at[1 + core], expert=far_chip + 1
        ),
    ]
    sib_copy(0, theirs).start()

    @pl.when(core == 0)
    def _():
        x_copy(0).start()

    for copy in meta_copies:
        copy.start()
    sib_copy(1, mine).start()
    sib_copy(0, mine).wait_recv()

    @pl.when(core == 1)
    def _():
        x_copy(0).start()

    x_copy(1).start()
    gate_copy(2).start()
    up_copy(2).start()

    def meta_arrived(slot):
        remote(
            meta.at[0], meta.at[slot], meta_s.at[0], meta_r.at[slot - 1], expert=sibling
        ).wait_recv()

    def gather(slot, place):
        expert = me.astype(F32)
        about = meta[slot]
        first = about[0:1, :] == expert
        second = about[1:2, :] == expert
        chosen = jnp.where(first, 1.0, 0.0) + jnp.where(second, 1.0, 0.0)
        weight = jnp.where(first, about[2:3, :], 0.0) + jnp.where(second, about[3:4, :], 0.0)
        upper = jnp.where(
            lax.broadcasted_iota(jnp.int32, (tokens, tokens), 0)
            < lax.broadcasted_iota(jnp.int32, (tokens, tokens), 1),
            1.0, 0.0,
        ).astype(BF16)
        ahead = jnp.dot(
            jnp.broadcast_to(chosen, (16, tokens)).astype(BF16), upper,
            preferred_element_type=F32,
        )[0:1, :]
        wanted = lax.broadcasted_iota(jnp.int32, (CAP, tokens), 0).astype(F32)
        picked = jnp.where(ahead == wanted, 1.0, 0.0) * chosen
        pick[place] = picked.astype(BF16)
        put[place] = picked.T.astype(BF16)
        scale[place] = jnp.broadcast_to(
            jnp.sum(picked * weight, axis=1, keepdims=True), (CAP, scale.shape[2])
        )

        @pl.loop(0, model // WIDE)
        def _(n):
            cols = pl.ds(pl.multiple_of(n * WIDE, WIDE), WIDE)
            rows_in[place * CAP:(place + 1) * CAP, cols] = jnp.dot(
                pick[place], nrm[slot, :, cols], preferred_element_type=F32
            ).astype(BF16)

    def up_tile(count, i):
        cols = pl.ds(pl.multiple_of(i * NARROW, NARROW), NARROW)
        gate = jnp.dot(rows_in[0:count, :], gate_w[:, cols], preferred_element_type=F32)
        upward = jnp.dot(rows_in[0:count, :], up_w[:, cols], preferred_element_type=F32)
        hidden[0:count, cols] = (jax.nn.silu(gate) * upward).astype(BF16)

    def spread(place, product):
        weighted = (
            product[place * CAP:(place + 1) * CAP, :] * scale[place][:, 0:1]
        ).astype(BF16)
        return jnp.dot(put[place], weighted, preferred_element_type=F32)

    def local_copy(n):
        return remote(
            local_out.at[n], local_in.at[n], local_s.at[n], local_r.at[n],
            expert=sibling,
        )

    def swap_copy(source, n):
        return remote(
            far_out.at[source, n, theirs], far_in.at[source, n],
            swap_s.at[source * tiles + n], swap_r.at[source * tiles + n], expert=sibling,
        )

    def back_copy(source, n):
        return remote(
            far_out.at[source, n, mine], back.at[n, mine],
            back_s.at[source * tiles + n], back_r.at[core * tiles + n],
            expert=far_chip + source,
        )

    def hand_copy(n):
        return remote(
            back.at[n], out.at[n], hand_s.at[n], hand_r.at[n], section=after
        )

    def settle(source, n):
        swap_copy(source, n).wait_recv()
        far_out[source, n, mine, :] = (
            far_out[source, n, mine, :].astype(F32) + far_in[source, n].astype(F32)
        ).astype(BF16)
        back_copy(source, n).start()

    def finish(n):
        local_copy(n).wait_recv()
        for sender in range(2):
            rows = pl.ds(sender * half, half)
            remote(
                back.at[n, rows], back.at[n, rows], back_s.at[0],
                back_r.at[sender * tiles + n], expert=far_chip,
            ).wait_recv()
        for first in range(0, tokens, 32):
            rows = pl.ds(first, 32)
            back[n, rows, :] = (
                base[n, rows, :] + local_in[n, rows, :].astype(F32)
                + back[n, rows, :].astype(F32)
            ).astype(BF16)
        hand_copy(n).start()

    def down_pass(source, extra):
        @pl.loop(0, tiles)
        def _(n):
            for part in range(WIDE // NARROW):
                cols = pl.ds(pl.multiple_of(n * WIDE + part * NARROW, NARROW), NARROW)
                product = jnp.dot(
                    hidden[0:CAP, :], down_w[:, cols], preferred_element_type=F32
                )
                part_cols = pl.ds(part * NARROW, NARROW)
                far_out[source, n, :, part_cols] = spread(0, product).astype(BF16)
            swap_copy(source, n).start()

            @pl.when(n >= LAG)
            def _():
                settle(source, n - LAG)

            extra(n)

        @pl.loop(tiles - LAG, tiles)
        def _(n):
            settle(source, n)

    gather(0, 0)
    sib_copy(1, theirs).wait_recv()
    meta_arrived(1)
    gather(1, 1)

    @pl.loop(0, UP_CHUNKS)
    def _(k):
        gate_copy(k).wait()
        up_copy(k).wait()

        @pl.when(k + 3 < UP_CHUNKS)
        def _():
            gate_copy(k + 3).start()
            up_copy(k + 3).start()

        @pl.when(k + 3 >= UP_CHUNKS)
        def _():
            down_copy(2 * (k + 3 - UP_CHUNKS)).start()
            down_copy(2 * (k + 3 - UP_CHUNKS) + 1).start()

        @pl.loop(0, up_width // NARROW)
        def _(i):
            up_tile(2 * CAP, k * (up_width // NARROW) + i)

    @pl.loop(0, tiles)
    def _(n):
        down_copy(n).wait()

        @pl.when(n + 6 < tiles)
        def _():
            down_copy(n + 6).start()

        for part in range(WIDE // NARROW):
            cols = pl.ds(pl.multiple_of(n * WIDE + part * NARROW, NARROW), NARROW)
            product = jnp.dot(hidden[...], down_w[:, cols], preferred_element_type=F32)
            part_cols = pl.ds(part * NARROW, NARROW)
            base[n, :, part_cols] = tok[:, cols].astype(F32) + spread(0, product)
            local_out[n, :, part_cols] = spread(1, product).astype(BF16)
        local_copy(n).start()

        @pl.when(n == 4)
        def _():
            x_copy(0).wait_recv()
            relay_copy(0, mine).start()

    meta_arrived(2)
    relay_copy(0, theirs).wait_recv()
    gather(2, 0)

    @pl.loop(0, units // NARROW)
    def _(i):
        up_tile(CAP, i)

    def relay_next(n):
        @pl.when(n == tiles - 2)
        def _():
            x_copy(1).wait_recv()
            relay_copy(1, mine).start()

    down_pass(0, relay_next)

    meta_arrived(3)
    relay_copy(1, theirs).wait_recv()
    gather(3, 0)
    early = units // NARROW // 2 - 1

    @pl.loop(0, units // NARROW)
    def _(i):
        up_tile(CAP, i)

        @pl.when((core == 0) & (i >= 2) & (lax.rem(i, 2) == 0))
        def _():
            finish(lax.div(i, 2) - 1)

    def hand_early(n):
        @pl.when((core == 0) & (n < 5) & (lax.rem(n, 2) == 0))
        def _():
            finish(early + lax.div(n, 2))

    down_pass(1, hand_early)

    @pl.when(core == 0)
    def _():
        @pl.loop(early + 3, tiles)
        def _(n):
            finish(n)

    @pl.when(core == 1)
    def _():
        @pl.loop(0, tiles)
        def _(n):
            finish(n)

    @pl.loop(0, tiles)
    def _(n):
        hand_copy(n).wait()
        local_copy(n).wait_send()
        for source in range(2):
            back_copy(source, n).wait_send()
            swap_copy(source, n).wait_send()

    for source in range(2):
        x_copy(source).wait_send()
        relay_copy(source, mine).wait_send()
    sib_copy(0, theirs).wait_send()
    sib_copy(1, mine).wait_send()
    for copy in meta_copies:
        copy.wait_send()


def copy_out(src, dst, held, in_sem, out_sem):
    ins, outs = [], []
    for n in range(src.shape[0]):
        cols = pl.ds(n * WIDE, WIDE)
        ins.append(pltpu.make_async_copy(src.at[n], held.at[n], in_sem.at[n]))
        outs.append(pltpu.make_async_copy(held.at[n], dst.at[:, cols], out_sem.at[n]))
    for copy in ins:
        copy.start()
    for n in range(src.shape[0]):
        ins[n].wait()
        outs[n].start()
    for copy in outs:
        copy.wait()


def two_chips(sections, tokens, norm_gain, expert_ids, gate_values, gate_weight, up_weight, down_weight):
    count, model = tokens.shape[1:]
    units = gate_weight.shape[2]
    half = count // 2
    tiles = model // WIDE
    rows = 2 * CAP
    dma = pltpu.SemaphoreType.DMA
    vmem = pl.BlockSpec(memory_space=pltpu.VMEM)
    hbm = pl.BlockSpec(memory_space=pl.ANY)
    handed = pl.pallas_call(
        functools.partial(kernel, sections),
        out_shape=jax.ShapeDtypeStruct((tiles, count, WIDE), BF16),
        in_specs=[vmem, vmem, vmem, vmem, hbm, hbm, hbm],
        out_specs=hbm,
        scratch_shapes=[
            pltpu.VMEM((model, units), BF16),
            pltpu.VMEM((model, units), BF16),
            pltpu.VMEM((units, model), BF16),
            pltpu.VMEM((4, count, model), BF16),
            pltpu.VMEM((4, 8, count), F32),
            pltpu.VMEM((2, CAP, count), BF16),
            pltpu.VMEM((2, count, CAP), BF16),
            pltpu.VMEM((2, CAP, 128), F32),
            pltpu.VMEM((rows, model), BF16),
            pltpu.VMEM((rows, units), BF16),
            pltpu.VMEM((tiles, count, WIDE), F32),
            pltpu.VMEM((tiles, count, WIDE), BF16),
            pltpu.VMEM((tiles, count, WIDE), BF16),
            pltpu.VMEM((2, tiles, count, WIDE), BF16),
            pltpu.VMEM((2, tiles, half, WIDE), BF16),
            pltpu.VMEM((tiles, count, WIDE), BF16),
            dma((2 * UP_CHUNKS + model // WIDE,)),
            dma((3,)), dma((3,)),
            dma((2,)), dma((2,)),
            dma((2,)), dma((2,)),
            dma((2,)), dma((2,)),
            dma((tiles,)), dma((tiles,)),
            dma((2 * tiles,)), dma((2 * tiles,)),
            dma((2 * tiles,)), dma((2 * tiles,)),
            dma((tiles,)), dma((tiles,)),
        ],
        compiler_params=pltpu.CompilerParams(
            collective_id=0, has_side_effects=True, vmem_limit_bytes=VMEM_LIMIT
        ),
        cost_estimate=pl.CostEstimate(
            flops=6 * EXPERTS * CAP * model * units, bytes_accessed=6 * model * units,
            transcendentals=EXPERTS * CAP * units,
        ),
    )(
        tokens[0], norm_gain, expert_ids[0].T, gate_values[0].T,
        gate_weight[0], up_weight[0], down_weight[0],
    )
    copied = pl.pallas_call(
        copy_out,
        out_shape=jax.ShapeDtypeStruct((count, model), BF16),
        in_specs=[hbm],
        out_specs=hbm,
        scratch_shapes=[pltpu.VMEM((tiles, count, WIDE), BF16), dma((tiles,)), dma((tiles,))],
        compiler_params=pltpu.CompilerParams(vmem_limit_bytes=VMEM_LIMIT),
        cost_estimate=pl.CostEstimate(
            flops=0, bytes_accessed=4 * count * model, transcendentals=0
        ),
    )(handed)
    return copied[None]


VMEM_LIMIT = 63 * 1024 * 1024


def shifted(shard, axis, by):
    devices = lax.axis_size(axis)
    return lax.ppermute(shard, axis, [(i, (i + by) % devices) for i in range(devices)])


def on_device(tokens, norm_gain, expert_ids, gate_values, gate_weight, up_weight, down_weight):
    resident = tokens[0]
    choice_ids = expert_ids[0]
    weights_in = gate_values[0]
    gate_local = gate_weight[0]
    up_local = up_weight[0]
    down_local = down_weight[0]
    owners = lax.axis_size("expert")
    shards = owners // EXPERTS
    tok_count = resident.shape[0]
    model_dim = resident.shape[1]
    capacity = CAP
    widened = resident.astype(jnp.float32)
    scale = lax.rsqrt(jnp.mean(widened * widened, axis=-1, keepdims=True) + 1e-06)
    normed = (widened * scale * norm_gain[0][None, :]).astype(jnp.bfloat16)
    flat_ids = choice_ids.reshape(-1)
    onehot = (flat_ids[:, None] == jnp.arange(EXPERTS, dtype=jnp.int32)[None, :]).astype(jnp.int32)
    position = jnp.cumsum(onehot, axis=0) - 1
    slot_of = jnp.sum(position * onehot, axis=1).reshape(tok_count, TOP)
    target = choice_ids * capacity + slot_of
    dispatch_matrix = jnp.sum(
        (
            target[:, :, None] == jnp.arange(EXPERTS * capacity, dtype=jnp.int32)[None, None, :]
        ).astype(jnp.bfloat16),
        axis=1,
    )
    outgoing = jnp.einsum(
        "tr,td->rd", dispatch_matrix, normed, preferred_element_type=jnp.float32
    ).astype(jnp.bfloat16)
    outgoing = jnp.repeat(outgoing.reshape(EXPERTS, capacity, model_dim), shards, axis=0)
    arrived = lax.all_to_all(outgoing, "expert", split_axis=0, concat_axis=0, tiled=True)
    sources = arrived.shape[0]
    count = arrived.shape[1]
    flat_rows = arrived.reshape(sources * count, model_dim)
    gate = jnp.dot(flat_rows, gate_local, preferred_element_type=jnp.float32)
    upward = jnp.dot(flat_rows, up_local, preferred_element_type=jnp.float32)
    hidden = (jax.nn.silu(gate) * upward).astype(jnp.bfloat16)
    partial_out = jnp.dot(hidden, down_local, preferred_element_type=jnp.float32).astype(
        jnp.bfloat16
    )
    partials = partial_out.reshape(sources, count, model_dim)
    returned = lax.all_to_all(partials, "expert", split_axis=0, concat_axis=0, tiled=True)
    summed = jnp.sum(
        returned.astype(jnp.float32).reshape(EXPERTS, shards, capacity, model_dim), axis=1
    )
    picked = summed.reshape(EXPERTS * capacity, model_dim)[target]
    mixture = jnp.sum(weights_in[:, :, None] * picked, axis=1)
    layer_out = (widened + mixture).astype(jnp.bfloat16)
    handed = shifted(layer_out, "section", 1)
    return handed[None]


def solution(mesh):
    in_specs = (
        P("section", "expert", None),
        P("section", None),
        P("section", "expert", None),
        P("section", "expert", None),
        P("section", None, "expert"),
        P("section", None, "expert"),
        P("section", "expert", None),
    )
    out_specs = P("section", "expert", None)
    if mesh.shape["expert"] == EXPERTS:
        on_one = functools.partial(two_chips, mesh.shape["section"])
    else:
        on_one = on_device
    return jax.shard_map(
        on_one, mesh=mesh, in_specs=in_specs, out_specs=out_specs, check_vma=False
    )
```

```python
import functools

import jax
import jax.numpy as jnp
from jax import lax
from jax.experimental import pallas as pl
from jax.experimental.pallas import tpu as pltpu
from jax.sharding import PartitionSpec as P

EXPERTS = 4
TOP = 2
CAP = 80
MESH = pl.DeviceIdType.MESH
F32 = jnp.float32
BF16 = jnp.bfloat16
UP_CHUNKS = 4
WIDE = 512
NARROW = 256
STEP = 16
LAG = 3


def kernel(
    sections, tok, gain, ids, gates, gate_hbm, up_hbm, down_hbm, out,
    gate_w, up_w, down_w, nrm, meta, pick, put, scale, rows_in, hidden, base, local_out, local_in,
    far_out, far_in, back,
    w_sem, meta_s, meta_r, sib_s, sib_r, x_s, x_r, relay_s, relay_r, local_s, local_r,
    swap_s, swap_r, back_s, back_r, hand_s, hand_r,
):
    tokens, model = tok.shape
    units = gate_w.shape[1]
    half = tokens // 2
    tiles = model // WIDE
    section = lax.axis_index("section")
    me = lax.axis_index("expert")
    chip = lax.div(me, 2)
    core = lax.rem(me, 2)
    other = 1 - core
    sibling = chip * 2 + other
    far_chip = (1 - chip) * 2
    after = lax.rem(section + 1, sections)
    before = lax.rem(section + sections - 1, sections)
    mine = pl.ds(pl.multiple_of(core * half, half), half)
    theirs = pl.ds(pl.multiple_of(other * half, half), half)

    def remote(src, dst, send, recv, **device):
        return pltpu.make_async_remote_copy(
            src_ref=src, dst_ref=dst, send_sem=send, recv_sem=recv,
            device_id=device, device_id_type=MESH,
        )

    barrier = pltpu.get_barrier_semaphore()
    for peer in (sibling, far_chip, far_chip + 1):
        pl.semaphore_signal(barrier, inc=1, device_id={"expert": peer}, device_id_type=MESH)
    for peer in (after, before):
        pl.semaphore_signal(barrier, inc=1, device_id={"section": peer}, device_id_type=MESH)

    up_width = units // UP_CHUNKS

    def gate_copy(k):
        cols = pl.ds(pl.multiple_of(k * up_width, up_width), up_width)
        return pltpu.make_async_copy(gate_hbm.at[:, cols], gate_w.at[:, cols], w_sem.at[k])

    def up_copy(k):
        cols = pl.ds(pl.multiple_of(k * up_width, up_width), up_width)
        return pltpu.make_async_copy(up_hbm.at[:, cols], up_w.at[:, cols], w_sem.at[UP_CHUNKS + k])

    def down_copy(k):
        cols = pl.ds(pl.multiple_of(k * WIDE, WIDE), WIDE)
        return pltpu.make_async_copy(
            down_hbm.at[:, cols], down_w.at[:, cols], w_sem.at[2 * UP_CHUNKS + k]
        )

    for k in range(2):
        gate_copy(k).start()
        up_copy(k).start()

    meta[0] = jnp.zeros(meta.shape[1:], F32)
    meta[0, 0:TOP, :] = ids[...].astype(F32)
    meta[0, TOP:2 * TOP, :] = gates[...]

    @pl.loop(0, tokens // STEP)
    def _(i):
        rows = pl.ds(pl.multiple_of(i * STEP, STEP), STEP)
        widened = tok[rows, :].astype(F32)
        inverse = lax.rsqrt(jnp.mean(widened * widened, axis=-1, keepdims=True) + 1e-06)
        nrm[0, rows, :] = (widened * inverse * gain[...]).astype(BF16)

    pl.semaphore_wait(barrier, 5)

    def sib_copy(k, rows):
        return remote(
            nrm.at[0, rows], nrm.at[1, rows], sib_s.at[k], sib_r.at[k], expert=sibling
        )

    def x_copy(source):
        slot = lax.rem(source + 2 - core, 2)
        return remote(
            nrm.at[slot, mine], nrm.at[2 + source, mine], x_s.at[source], x_r.at[source],
            expert=far_chip + core,
        )

    def relay_copy(source, rows):
        return remote(
            nrm.at[2 + source, rows], nrm.at[2 + source, rows], relay_s.at[source],
            relay_r.at[source], expert=sibling,
        )

    meta_copies = [
        remote(meta.at[0], meta.at[1], meta_s.at[0], meta_r.at[0], expert=sibling),
        remote(meta.at[0], meta.at[2 + core], meta_s.at[1], meta_r.at[1 + core], expert=far_chip),
        remote(
            meta.at[0], meta.at[2 + core], meta_s.at[2], meta_r.at[1 + core], expert=far_chip + 1
        ),
    ]
    sib_copy(0, theirs).start()

    @pl.when(core == 0)
    def _():
        x_copy(0).start()

    for copy in meta_copies:
        copy.start()
    sib_copy(1, mine).start()
    sib_copy(0, mine).wait_recv()

    @pl.when(core == 1)
    def _():
        x_copy(0).start()

    gate_copy(2).start()
    up_copy(2).start()

    def meta_arrived(slot):
        remote(
            meta.at[0], meta.at[slot], meta_s.at[0], meta_r.at[slot - 1], expert=sibling
        ).wait_recv()

    def gather(slot, place):
        expert = me.astype(F32)
        about = meta[slot]
        first = about[0:1, :] == expert
        second = about[1:2, :] == expert
        chosen = jnp.where(first, 1.0, 0.0) + jnp.where(second, 1.0, 0.0)
        weight = jnp.where(first, about[2:3, :], 0.0) + jnp.where(second, about[3:4, :], 0.0)
        upper = jnp.where(
            lax.broadcasted_iota(jnp.int32, (tokens, tokens), 0)
            < lax.broadcasted_iota(jnp.int32, (tokens, tokens), 1),
            1.0, 0.0,
        ).astype(BF16)
        ahead = jnp.dot(
            jnp.broadcast_to(chosen, (16, tokens)).astype(BF16), upper,
            preferred_element_type=F32,
        )[0:1, :]
        wanted = lax.broadcasted_iota(jnp.int32, (CAP, tokens), 0).astype(F32)
        picked = jnp.where(ahead == wanted, 1.0, 0.0) * chosen
        pick[place] = picked.astype(BF16)
        put[place] = picked.T.astype(BF16)
        scale[place] = jnp.broadcast_to(
            jnp.sum(picked * weight, axis=1, keepdims=True), (CAP, scale.shape[2])
        )

        @pl.loop(0, model // WIDE)
        def _(n):
            cols = pl.ds(pl.multiple_of(n * WIDE, WIDE), WIDE)
            rows_in[place * CAP:(place + 1) * CAP, cols] = jnp.dot(
                pick[place], nrm[slot, :, cols], preferred_element_type=F32
            ).astype(BF16)

    def up_tile(count, i):
        cols = pl.ds(pl.multiple_of(i * NARROW, NARROW), NARROW)
        gate = jnp.dot(rows_in[0:count, :], gate_w[:, cols], preferred_element_type=F32)
        upward = jnp.dot(rows_in[0:count, :], up_w[:, cols], preferred_element_type=F32)
        hidden[0:count, cols] = (jax.nn.silu(gate) * upward).astype(BF16)

    def spread(place, product):
        weighted = (
            product[place * CAP:(place + 1) * CAP, :] * scale[place][:, 0:1]
        ).astype(BF16)
        return jnp.dot(put[place], weighted, preferred_element_type=F32)

    def local_copy(n):
        return remote(
            local_out.at[n], local_in.at[n], local_s.at[n], local_r.at[n],
            expert=sibling,
        )

    def swap_copy(source, n):
        return remote(
            far_out.at[source, n, theirs], far_in.at[source, n],
            swap_s.at[source * tiles + n], swap_r.at[source * tiles + n], expert=sibling,
        )

    def back_copy(source, n):
        return remote(
            far_out.at[source, n, mine], back.at[n, mine],
            back_s.at[source * tiles + n], back_r.at[core * tiles + n],
            expert=far_chip + source,
        )

    def hand_copy(n):
        return remote(
            back.at[n], out.at[n], hand_s.at[n], hand_r.at[n], section=after
        )

    def settle(source, n):
        swap_copy(source, n).wait_recv()
        far_out[source, n, mine, :] = (
            far_out[source, n, mine, :].astype(F32) + far_in[source, n].astype(F32)
        ).astype(BF16)
        back_copy(source, n).start()

    def finish(n):
        local_copy(n).wait_recv()
        for sender in range(2):
            rows = pl.ds(sender * half, half)
            remote(
                back.at[n, rows], back.at[n, rows], back_s.at[0],
                back_r.at[sender * tiles + n], expert=far_chip,
            ).wait_recv()
        for first in range(0, tokens, 32):
            rows = pl.ds(first, 32)
            back[n, rows, :] = (
                base[n, rows, :] + local_in[n, rows, :].astype(F32)
                + back[n, rows, :].astype(F32)
            ).astype(BF16)
        hand_copy(n).start()

    def down_pass(source, extra):
        @pl.loop(0, tiles)
        def _(n):
            for part in range(WIDE // NARROW):
                cols = pl.ds(pl.multiple_of(n * WIDE + part * NARROW, NARROW), NARROW)
                product = jnp.dot(
                    hidden[0:CAP, :], down_w[:, cols], preferred_element_type=F32
                )
                part_cols = pl.ds(part * NARROW, NARROW)
                far_out[source, n, :, part_cols] = spread(0, product).astype(BF16)
            swap_copy(source, n).start()

            @pl.when((n >= 2) & (n < 2 + 2 * LAG) & (lax.rem(n, 2) == 0))
            def _():
                settle(source, lax.div(n, 2) - 1)

            extra(n)

    gather(0, 0)
    sib_copy(1, theirs).wait_recv()
    meta_arrived(1)
    gather(1, 1)

    @pl.loop(0, UP_CHUNKS)
    def _(k):
        gate_copy(k).wait()
        up_copy(k).wait()

        @pl.when(k == UP_CHUNKS - 1)
        def _():
            x_copy(0).wait_send()
            x_copy(1).start()

        @pl.when(k + 3 < UP_CHUNKS)
        def _():
            gate_copy(k + 3).start()
            up_copy(k + 3).start()

        @pl.when(k + 3 >= UP_CHUNKS)
        def _():
            down_copy(2 * (k + 3 - UP_CHUNKS)).start()
            down_copy(2 * (k + 3 - UP_CHUNKS) + 1).start()

        @pl.loop(0, up_width // NARROW)
        def _(i):
            up_tile(2 * CAP, k * (up_width // NARROW) + i)

    @pl.loop(0, tiles)
    def _(n):
        down_copy(n).wait()

        @pl.when(n + 6 < tiles)
        def _():
            down_copy(n + 6).start()

        for part in range(WIDE // NARROW):
            cols = pl.ds(pl.multiple_of(n * WIDE + part * NARROW, NARROW), NARROW)
            product = jnp.dot(hidden[...], down_w[:, cols], preferred_element_type=F32)
            part_cols = pl.ds(part * NARROW, NARROW)
            base[n, :, part_cols] = tok[:, cols].astype(F32) + spread(0, product)
            local_out[n, :, part_cols] = spread(1, product).astype(BF16)
        local_copy(n).start()

        @pl.when(n == 1)
        def _():
            x_copy(0).wait_recv()
            relay_copy(0, mine).start()

    meta_arrived(2)
    relay_copy(0, theirs).wait_recv()
    gather(2, 0)

    @pl.loop(0, units // NARROW)
    def _(i):
        up_tile(CAP, i)

    def relay_next(n):
        @pl.when(n == 1)
        def _():
            x_copy(1).wait_recv()
            relay_copy(1, mine).start()

    down_pass(0, relay_next)

    meta_arrived(3)
    relay_copy(1, theirs).wait_recv()
    gather(3, 0)
    slots = units // NARROW

    def settle_next(source, n):
        back_copy(source, n - 2).wait_send()
        settle(source, n)

    @pl.loop(0, slots)
    def _(i):
        up_tile(CAP, i)

        @pl.when(i < tiles - LAG)
        def _():
            settle_next(0, i + LAG)

        @pl.when((core == 0) & (i >= 3))
        def _():
            finish(i - 3)

    def hand_early(n):
        @pl.when((core == 0) & (n < 2 * (tiles - slots + 3)) & (lax.rem(n, 2) == 0))
        def _():
            finish(slots - 3 + lax.div(n, 2))

    down_pass(1, hand_early)

    @pl.loop(LAG, tiles)
    def _(n):
        settle_next(1, n)

        @pl.when(core == 1)
        def _():
            finish(n - LAG)

    @pl.when(core == 1)
    def _():
        @pl.loop(tiles - LAG, tiles)
        def _(n):
            finish(n)

    @pl.loop(0, tiles)
    def _(n):
        hand_copy(n).wait()
        local_copy(n).wait_send()
        for source in range(2):
            swap_copy(source, n).wait_send()

            @pl.when((n < LAG - 2) | (n >= tiles - 2))
            def _():
                back_copy(source, n).wait_send()

    for source in range(2):
        relay_copy(source, mine).wait_send()
    x_copy(1).wait_send()
    sib_copy(0, theirs).wait_send()
    sib_copy(1, mine).wait_send()
    for copy in meta_copies:
        copy.wait_send()


def copy_out(src, dst, held, in_sem, out_sem):
    ins, outs = [], []
    for n in range(src.shape[0]):
        cols = pl.ds(n * WIDE, WIDE)
        ins.append(pltpu.make_async_copy(src.at[n], held.at[n], in_sem.at[n]))
        outs.append(pltpu.make_async_copy(held.at[n], dst.at[:, cols], out_sem.at[n]))
    for copy in ins:
        copy.start()
    for n in range(src.shape[0]):
        ins[n].wait()
        outs[n].start()
    for copy in outs:
        copy.wait()


def two_chips(sections, tokens, norm_gain, expert_ids, gate_values, gate_weight, up_weight, down_weight):
    count, model = tokens.shape[1:]
    units = gate_weight.shape[2]
    half = count // 2
    tiles = model // WIDE
    rows = 2 * CAP
    dma = pltpu.SemaphoreType.DMA
    vmem = pl.BlockSpec(memory_space=pltpu.VMEM)
    hbm = pl.BlockSpec(memory_space=pl.ANY)
    handed = pl.pallas_call(
        functools.partial(kernel, sections),
        out_shape=jax.ShapeDtypeStruct((tiles, count, WIDE), BF16),
        in_specs=[vmem, vmem, vmem, vmem, hbm, hbm, hbm],
        out_specs=hbm,
        scratch_shapes=[
            pltpu.VMEM((model, units), BF16),
            pltpu.VMEM((model, units), BF16),
            pltpu.VMEM((units, model), BF16),
            pltpu.VMEM((4, count, model), BF16),
            pltpu.VMEM((4, 8, count), F32),
            pltpu.VMEM((2, CAP, count), BF16),
            pltpu.VMEM((2, count, CAP), BF16),
            pltpu.VMEM((2, CAP, 128), F32),
            pltpu.VMEM((rows, model), BF16),
            pltpu.VMEM((rows, units), BF16),
            pltpu.VMEM((tiles, count, WIDE), F32),
            pltpu.VMEM((tiles, count, WIDE), BF16),
            pltpu.VMEM((tiles, count, WIDE), BF16),
            pltpu.VMEM((2, tiles, count, WIDE), BF16),
            pltpu.VMEM((2, tiles, half, WIDE), BF16),
            pltpu.VMEM((tiles, count, WIDE), BF16),
            dma((2 * UP_CHUNKS + model // WIDE,)),
            dma((3,)), dma((3,)),
            dma((2,)), dma((2,)),
            dma((2,)), dma((2,)),
            dma((2,)), dma((2,)),
            dma((tiles,)), dma((tiles,)),
            dma((2 * tiles,)), dma((2 * tiles,)),
            dma((2 * tiles,)), dma((2 * tiles,)),
            dma((tiles,)), dma((tiles,)),
        ],
        compiler_params=pltpu.CompilerParams(
            collective_id=0, has_side_effects=True, vmem_limit_bytes=VMEM_LIMIT
        ),
        cost_estimate=pl.CostEstimate(
            flops=6 * EXPERTS * CAP * model * units, bytes_accessed=6 * model * units,
            transcendentals=EXPERTS * CAP * units,
        ),
    )(
        tokens[0], norm_gain, expert_ids[0].T, gate_values[0].T,
        gate_weight[0], up_weight[0], down_weight[0],
    )
    copied = pl.pallas_call(
        copy_out,
        out_shape=jax.ShapeDtypeStruct((count, model), BF16),
        in_specs=[hbm],
        out_specs=hbm,
        scratch_shapes=[pltpu.VMEM((tiles, count, WIDE), BF16), dma((tiles,)), dma((tiles,))],
        compiler_params=pltpu.CompilerParams(vmem_limit_bytes=VMEM_LIMIT),
        cost_estimate=pl.CostEstimate(
            flops=0, bytes_accessed=4 * count * model, transcendentals=0
        ),
    )(handed)
    return copied[None]


VMEM_LIMIT = 63 * 1024 * 1024


def shifted(shard, axis, by):
    devices = lax.axis_size(axis)
    return lax.ppermute(shard, axis, [(i, (i + by) % devices) for i in range(devices)])


def on_device(tokens, norm_gain, expert_ids, gate_values, gate_weight, up_weight, down_weight):
    resident = tokens[0]
    choice_ids = expert_ids[0]
    weights_in = gate_values[0]
    gate_local = gate_weight[0]
    up_local = up_weight[0]
    down_local = down_weight[0]
    owners = lax.axis_size("expert")
    shards = owners // EXPERTS
    tok_count = resident.shape[0]
    model_dim = resident.shape[1]
    capacity = CAP
    widened = resident.astype(jnp.float32)
    scale = lax.rsqrt(jnp.mean(widened * widened, axis=-1, keepdims=True) + 1e-06)
    normed = (widened * scale * norm_gain[0][None, :]).astype(jnp.bfloat16)
    flat_ids = choice_ids.reshape(-1)
    onehot = (flat_ids[:, None] == jnp.arange(EXPERTS, dtype=jnp.int32)[None, :]).astype(jnp.int32)
    position = jnp.cumsum(onehot, axis=0) - 1
    slot_of = jnp.sum(position * onehot, axis=1).reshape(tok_count, TOP)
    target = choice_ids * capacity + slot_of
    dispatch_matrix = jnp.sum(
        (
            target[:, :, None] == jnp.arange(EXPERTS * capacity, dtype=jnp.int32)[None, None, :]
        ).astype(jnp.bfloat16),
        axis=1,
    )
    outgoing = jnp.einsum(
        "tr,td->rd", dispatch_matrix, normed, preferred_element_type=jnp.float32
    ).astype(jnp.bfloat16)
    outgoing = jnp.repeat(outgoing.reshape(EXPERTS, capacity, model_dim), shards, axis=0)
    arrived = lax.all_to_all(outgoing, "expert", split_axis=0, concat_axis=0, tiled=True)
    sources = arrived.shape[0]
    count = arrived.shape[1]
    flat_rows = arrived.reshape(sources * count, model_dim)
    gate = jnp.dot(flat_rows, gate_local, preferred_element_type=jnp.float32)
    upward = jnp.dot(flat_rows, up_local, preferred_element_type=jnp.float32)
    hidden = (jax.nn.silu(gate) * upward).astype(jnp.bfloat16)
    partial_out = jnp.dot(hidden, down_local, preferred_element_type=jnp.float32).astype(
        jnp.bfloat16
    )
    partials = partial_out.reshape(sources, count, model_dim)
    returned = lax.all_to_all(partials, "expert", split_axis=0, concat_axis=0, tiled=True)
    summed = jnp.sum(
        returned.astype(jnp.float32).reshape(EXPERTS, shards, capacity, model_dim), axis=1
    )
    picked = summed.reshape(EXPERTS * capacity, model_dim)[target]
    mixture = jnp.sum(weights_in[:, :, None] * picked, axis=1)
    layer_out = (widened + mixture).astype(jnp.bfloat16)
    handed = shifted(layer_out, "section", 1)
    return handed[None]


def solution(mesh):
    in_specs = (
        P("section", "expert", None),
        P("section", None),
        P("section", "expert", None),
        P("section", "expert", None),
        P("section", None, "expert"),
        P("section", None, "expert"),
        P("section", "expert", None),
    )
    out_specs = P("section", "expert", None)
    if mesh.shape["expert"] == EXPERTS:
        on_one = functools.partial(two_chips, mesh.shape["section"])
    else:
        on_one = on_device
    return jax.shard_map(
        on_one, mesh=mesh, in_specs=in_specs, out_specs=out_specs, check_vma=False
    )
```

```python
import functools

import jax
import jax.numpy as jnp
from jax import lax
from jax.experimental import pallas as pl
from jax.experimental.pallas import tpu as pltpu
from jax.sharding import PartitionSpec as P

EXPERTS = 4
TOP = 2
CAP = 80
MESH = pl.DeviceIdType.MESH
F32 = jnp.float32
BF16 = jnp.bfloat16
UP_CHUNKS = 4
WIDE = 512
NARROW = 512
STEP = 16
LAG = 3


def kernel(
    sections, tok, gain, ids, gates, gate_hbm, up_hbm, down_hbm, out,
    gate_w, up_w, down_w, nrm, meta, pick, put, scale, rows_in, hidden, base, local_out, local_in,
    far_out, far_in, back,
    w_sem, meta_s, meta_r, sib_s, sib_r, x_s, x_r, relay_s, relay_r, local_s, local_r,
    swap_s, swap_r, back_s, back_r, hand_s, hand_r,
):
    tokens, model = tok.shape
    units = gate_w.shape[1]
    half = tokens // 2
    tiles = model // WIDE
    section = lax.axis_index("section")
    me = lax.axis_index("expert")
    chip = lax.div(me, 2)
    core = lax.rem(me, 2)
    other = 1 - core
    sibling = chip * 2 + other
    far_chip = (1 - chip) * 2
    after = lax.rem(section + 1, sections)
    before = lax.rem(section + sections - 1, sections)
    mine = pl.ds(pl.multiple_of(core * half, half), half)
    theirs = pl.ds(pl.multiple_of(other * half, half), half)

    def remote(src, dst, send, recv, **device):
        return pltpu.make_async_remote_copy(
            src_ref=src, dst_ref=dst, send_sem=send, recv_sem=recv,
            device_id=device, device_id_type=MESH,
        )

    barrier = pltpu.get_barrier_semaphore()
    for peer in (sibling, far_chip, far_chip + 1):
        pl.semaphore_signal(barrier, inc=1, device_id={"expert": peer}, device_id_type=MESH)
    for peer in (after, before):
        pl.semaphore_signal(barrier, inc=1, device_id={"section": peer}, device_id_type=MESH)

    up_width = units // UP_CHUNKS

    def gate_copy(k):
        cols = pl.ds(pl.multiple_of(k * up_width, up_width), up_width)
        return pltpu.make_async_copy(gate_hbm.at[:, cols], gate_w.at[:, cols], w_sem.at[k])

    def up_copy(k):
        cols = pl.ds(pl.multiple_of(k * up_width, up_width), up_width)
        return pltpu.make_async_copy(up_hbm.at[:, cols], up_w.at[:, cols], w_sem.at[UP_CHUNKS + k])

    def down_copy(k):
        cols = pl.ds(pl.multiple_of(k * WIDE, WIDE), WIDE)
        return pltpu.make_async_copy(
            down_hbm.at[:, cols], down_w.at[:, cols], w_sem.at[2 * UP_CHUNKS + k]
        )

    for k in range(2):
        gate_copy(k).start()
        up_copy(k).start()

    meta[0] = jnp.zeros(meta.shape[1:], F32)
    meta[0, 0:TOP, :] = ids[...].astype(F32)
    meta[0, TOP:2 * TOP, :] = gates[...]

    @pl.loop(0, tokens // STEP)
    def _(i):
        rows = pl.ds(pl.multiple_of(i * STEP, STEP), STEP)
        widened = tok[rows, :].astype(F32)
        inverse = lax.rsqrt(jnp.mean(widened * widened, axis=-1, keepdims=True) + 1e-06)
        nrm[0, rows, :] = (widened * inverse * gain[...]).astype(BF16)

    pl.semaphore_wait(barrier, 5)

    def sib_copy(k, rows):
        return remote(
            nrm.at[0, rows], nrm.at[1, rows], sib_s.at[k], sib_r.at[k], expert=sibling
        )

    def x_copy(source):
        slot = lax.rem(source + 2 - core, 2)
        return remote(
            nrm.at[slot, mine], nrm.at[2 + source, mine], x_s.at[source], x_r.at[source],
            expert=far_chip + core,
        )

    def relay_copy(source, rows):
        return remote(
            nrm.at[2 + source, rows], nrm.at[2 + source, rows], relay_s.at[source],
            relay_r.at[source], expert=sibling,
        )

    meta_copies = [
        remote(meta.at[0], meta.at[1], meta_s.at[0], meta_r.at[0], expert=sibling),
        remote(meta.at[0], meta.at[2 + core], meta_s.at[1], meta_r.at[1 + core], expert=far_chip),
        remote(
            meta.at[0], meta.at[2 + core], meta_s.at[2], meta_r.at[1 + core], expert=far_chip + 1
        ),
    ]
    sib_copy(0, theirs).start()

    @pl.when(core == 0)
    def _():
        x_copy(0).start()

    for copy in meta_copies:
        copy.start()
    sib_copy(1, mine).start()
    sib_copy(0, mine).wait_recv()

    @pl.when(core == 1)
    def _():
        x_copy(0).start()

    gate_copy(2).start()
    up_copy(2).start()

    def meta_arrived(slot):
        remote(
            meta.at[0], meta.at[slot], meta_s.at[0], meta_r.at[slot - 1], expert=sibling
        ).wait_recv()

    def gather(slot, place):
        expert = me.astype(F32)
        about = meta[slot]
        first = about[0:1, :] == expert
        second = about[1:2, :] == expert
        chosen = jnp.where(first, 1.0, 0.0) + jnp.where(second, 1.0, 0.0)
        weight = jnp.where(first, about[2:3, :], 0.0) + jnp.where(second, about[3:4, :], 0.0)
        upper = jnp.where(
            lax.broadcasted_iota(jnp.int32, (tokens, tokens), 0)
            < lax.broadcasted_iota(jnp.int32, (tokens, tokens), 1),
            1.0, 0.0,
        ).astype(BF16)
        ahead = jnp.dot(
            jnp.broadcast_to(chosen, (16, tokens)).astype(BF16), upper,
            preferred_element_type=F32,
        )[0:1, :]
        wanted = lax.broadcasted_iota(jnp.int32, (CAP, tokens), 0).astype(F32)
        picked = jnp.where(ahead == wanted, 1.0, 0.0) * chosen
        pick[place] = picked.astype(BF16)
        put[place] = picked.T.astype(BF16)
        scale[place] = jnp.broadcast_to(
            jnp.sum(picked * weight, axis=1, keepdims=True), (CAP, scale.shape[2])
        )

        @pl.loop(0, model // WIDE)
        def _(n):
            cols = pl.ds(pl.multiple_of(n * WIDE, WIDE), WIDE)
            rows_in[place * CAP:(place + 1) * CAP, cols] = jnp.dot(
                pick[place], nrm[slot, :, cols], preferred_element_type=F32
            ).astype(BF16)

    def up_tile(count, i):
        cols = pl.ds(pl.multiple_of(i * NARROW, NARROW), NARROW)
        gate = jnp.dot(rows_in[0:count, :], gate_w[:, cols], preferred_element_type=F32)
        upward = jnp.dot(rows_in[0:count, :], up_w[:, cols], preferred_element_type=F32)
        hidden[0:count, cols] = (jax.nn.silu(gate) * upward).astype(BF16)

    def spread(place, product):
        weighted = (
            product[place * CAP:(place + 1) * CAP, :] * scale[place][:, 0:1]
        ).astype(BF16)
        return jnp.dot(put[place], weighted, preferred_element_type=F32)

    def local_copy(n):
        return remote(
            local_out.at[n], local_in.at[n], local_s.at[n], local_r.at[n],
            expert=sibling,
        )

    def swap_copy(source, n):
        return remote(
            far_out.at[source, n, theirs], far_in.at[source, n],
            swap_s.at[source * tiles + n], swap_r.at[source * tiles + n], expert=sibling,
        )

    def back_copy(source, n):
        return remote(
            far_out.at[source, n, mine], back.at[n, mine],
            back_s.at[source * tiles + n], back_r.at[core * tiles + n],
            expert=far_chip + source,
        )

    def hand_copy(n):
        return remote(
            back.at[n], out.at[n], hand_s.at[n], hand_r.at[n], section=after
        )

    def settle(source, n):
        swap_copy(source, n).wait_recv()
        far_out[source, n, mine, :] = (
            far_out[source, n, mine, :].astype(F32) + far_in[source, n].astype(F32)
        ).astype(BF16)
        back_copy(source, n).start()

    def finish(n):
        local_copy(n).wait_recv()
        for sender in range(2):
            rows = pl.ds(sender * half, half)
            remote(
                back.at[n, rows], back.at[n, rows], back_s.at[0],
                back_r.at[sender * tiles + n], expert=far_chip,
            ).wait_recv()
        for first in range(0, tokens, 32):
            rows = pl.ds(first, 32)
            back[n, rows, :] = (
                base[n, rows, :] + local_in[n, rows, :].astype(F32)
                + back[n, rows, :].astype(F32)
            ).astype(BF16)
        hand_copy(n).start()

    def down_pass(source, extra):
        @pl.loop(0, tiles)
        def _(n):
            for part in range(WIDE // NARROW):
                cols = pl.ds(pl.multiple_of(n * WIDE + part * NARROW, NARROW), NARROW)
                product = jnp.dot(
                    hidden[0:CAP, :], down_w[:, cols], preferred_element_type=F32
                )
                part_cols = pl.ds(part * NARROW, NARROW)
                far_out[source, n, :, part_cols] = spread(0, product).astype(BF16)
            swap_copy(source, n).start()

            @pl.when((n >= 2) & (n < 2 + 2 * LAG) & (lax.rem(n, 2) == 0))
            def _():
                settle(source, lax.div(n, 2) - 1)

            extra(n)

    gather(0, 0)
    sib_copy(1, theirs).wait_recv()
    meta_arrived(1)
    gather(1, 1)

    @pl.loop(0, UP_CHUNKS)
    def _(k):
        gate_copy(k).wait()
        up_copy(k).wait()

        @pl.when(k == UP_CHUNKS - 1)
        def _():
            x_copy(0).wait_send()
            x_copy(1).start()

        @pl.when(k + 3 < UP_CHUNKS)
        def _():
            gate_copy(k + 3).start()
            up_copy(k + 3).start()

        @pl.when(k + 3 >= UP_CHUNKS)
        def _():
            down_copy(2 * (k + 3 - UP_CHUNKS)).start()
            down_copy(2 * (k + 3 - UP_CHUNKS) + 1).start()

        @pl.loop(0, up_width // NARROW)
        def _(i):
            up_tile(2 * CAP, k * (up_width // NARROW) + i)

    @pl.loop(0, tiles)
    def _(n):
        down_copy(n).wait()

        @pl.when(n + 6 < tiles)
        def _():
            down_copy(n + 6).start()

        for part in range(WIDE // NARROW):
            cols = pl.ds(pl.multiple_of(n * WIDE + part * NARROW, NARROW), NARROW)
            product = jnp.dot(hidden[...], down_w[:, cols], preferred_element_type=F32)
            part_cols = pl.ds(part * NARROW, NARROW)
            base[n, :, part_cols] = tok[:, cols].astype(F32) + spread(0, product)
            local_out[n, :, part_cols] = spread(1, product).astype(BF16)
        local_copy(n).start()

        @pl.when(n == 1)
        def _():
            x_copy(0).wait_recv()
            relay_copy(0, mine).start()

    meta_arrived(2)
    relay_copy(0, theirs).wait_recv()
    gather(2, 0)

    @pl.loop(0, units // NARROW)
    def _(i):
        up_tile(CAP, i)

    def relay_next(n):
        @pl.when(n == 1)
        def _():
            x_copy(1).wait_recv()
            relay_copy(1, mine).start()

    down_pass(0, relay_next)

    meta_arrived(3)
    relay_copy(1, theirs).wait_recv()
    gather(3, 0)
    slots = units // NARROW

    def settle_next(source, n):
        back_copy(source, n - 2).wait_send()
        settle(source, n)

    @pl.loop(0, slots)
    def _(i):
        up_tile(CAP, i)

        @pl.when(i < tiles - LAG)
        def _():
            settle_next(0, i + LAG)

        @pl.when((core == 0) & (i >= 2))
        def _():
            finish(i - 2)

    def hand_early(n):
        @pl.when((core == 0) & (n < tiles - slots + 2))
        def _():
            finish(slots - 2 + n)

    down_pass(1, hand_early)

    @pl.loop(LAG, tiles)
    def _(n):
        settle_next(1, n)

        @pl.when(core == 1)
        def _():
            finish(n - LAG)

    @pl.when(core == 1)
    def _():
        @pl.loop(tiles - LAG, tiles)
        def _(n):
            finish(n)

    @pl.loop(0, tiles)
    def _(n):
        hand_copy(n).wait()
        local_copy(n).wait_send()
        for source in range(2):
            swap_copy(source, n).wait_send()

            @pl.when((n < LAG - 2) | (n >= tiles - 2))
            def _():
                back_copy(source, n).wait_send()

    for source in range(2):
        relay_copy(source, mine).wait_send()
    x_copy(1).wait_send()
    sib_copy(0, theirs).wait_send()
    sib_copy(1, mine).wait_send()
    for copy in meta_copies:
        copy.wait_send()


def copy_out(src, dst, held, in_sem, out_sem):
    ins, outs = [], []
    for n in range(src.shape[0]):
        cols = pl.ds(n * WIDE, WIDE)
        ins.append(pltpu.make_async_copy(src.at[n], held.at[n], in_sem.at[n]))
        outs.append(pltpu.make_async_copy(held.at[n], dst.at[:, cols], out_sem.at[n]))
    for copy in ins:
        copy.start()
    for n in range(src.shape[0]):
        ins[n].wait()
        outs[n].start()
    for copy in outs:
        copy.wait()


def two_chips(sections, tokens, norm_gain, expert_ids, gate_values, gate_weight, up_weight, down_weight):
    count, model = tokens.shape[1:]
    units = gate_weight.shape[2]
    half = count // 2
    tiles = model // WIDE
    rows = 2 * CAP
    dma = pltpu.SemaphoreType.DMA
    vmem = pl.BlockSpec(memory_space=pltpu.VMEM)
    hbm = pl.BlockSpec(memory_space=pl.ANY)
    handed = pl.pallas_call(
        functools.partial(kernel, sections),
        out_shape=jax.ShapeDtypeStruct((tiles, count, WIDE), BF16),
        in_specs=[vmem, vmem, vmem, vmem, hbm, hbm, hbm],
        out_specs=hbm,
        scratch_shapes=[
            pltpu.VMEM((model, units), BF16),
            pltpu.VMEM((model, units), BF16),
            pltpu.VMEM((units, model), BF16),
            pltpu.VMEM((4, count, model), BF16),
            pltpu.VMEM((4, 8, count), F32),
            pltpu.VMEM((2, CAP, count), BF16),
            pltpu.VMEM((2, count, CAP), BF16),
            pltpu.VMEM((2, CAP, 128), F32),
            pltpu.VMEM((rows, model), BF16),
            pltpu.VMEM((rows, units), BF16),
            pltpu.VMEM((tiles, count, WIDE), F32),
            pltpu.VMEM((tiles, count, WIDE), BF16),
            pltpu.VMEM((tiles, count, WIDE), BF16),
            pltpu.VMEM((2, tiles, count, WIDE), BF16),
            pltpu.VMEM((2, tiles, half, WIDE), BF16),
            pltpu.VMEM((tiles, count, WIDE), BF16),
            dma((2 * UP_CHUNKS + model // WIDE,)),
            dma((3,)), dma((3,)),
            dma((2,)), dma((2,)),
            dma((2,)), dma((2,)),
            dma((2,)), dma((2,)),
            dma((tiles,)), dma((tiles,)),
            dma((2 * tiles,)), dma((2 * tiles,)),
            dma((2 * tiles,)), dma((2 * tiles,)),
            dma((tiles,)), dma((tiles,)),
        ],
        compiler_params=pltpu.CompilerParams(
            collective_id=0, has_side_effects=True, vmem_limit_bytes=VMEM_LIMIT
        ),
        cost_estimate=pl.CostEstimate(
            flops=6 * EXPERTS * CAP * model * units, bytes_accessed=6 * model * units,
            transcendentals=EXPERTS * CAP * units,
        ),
    )(
        tokens[0], norm_gain, expert_ids[0].T, gate_values[0].T,
        gate_weight[0], up_weight[0], down_weight[0],
    )
    copied = pl.pallas_call(
        copy_out,
        out_shape=jax.ShapeDtypeStruct((count, model), BF16),
        in_specs=[hbm],
        out_specs=hbm,
        scratch_shapes=[pltpu.VMEM((tiles, count, WIDE), BF16), dma((tiles,)), dma((tiles,))],
        compiler_params=pltpu.CompilerParams(vmem_limit_bytes=VMEM_LIMIT),
        cost_estimate=pl.CostEstimate(
            flops=0, bytes_accessed=4 * count * model, transcendentals=0
        ),
    )(handed)
    return copied[None]


VMEM_LIMIT = 63 * 1024 * 1024


def shifted(shard, axis, by):
    devices = lax.axis_size(axis)
    return lax.ppermute(shard, axis, [(i, (i + by) % devices) for i in range(devices)])


def on_device(tokens, norm_gain, expert_ids, gate_values, gate_weight, up_weight, down_weight):
    resident = tokens[0]
    choice_ids = expert_ids[0]
    weights_in = gate_values[0]
    gate_local = gate_weight[0]
    up_local = up_weight[0]
    down_local = down_weight[0]
    owners = lax.axis_size("expert")
    shards = owners // EXPERTS
    tok_count = resident.shape[0]
    model_dim = resident.shape[1]
    capacity = CAP
    widened = resident.astype(jnp.float32)
    scale = lax.rsqrt(jnp.mean(widened * widened, axis=-1, keepdims=True) + 1e-06)
    normed = (widened * scale * norm_gain[0][None, :]).astype(jnp.bfloat16)
    flat_ids = choice_ids.reshape(-1)
    onehot = (flat_ids[:, None] == jnp.arange(EXPERTS, dtype=jnp.int32)[None, :]).astype(jnp.int32)
    position = jnp.cumsum(onehot, axis=0) - 1
    slot_of = jnp.sum(position * onehot, axis=1).reshape(tok_count, TOP)
    target = choice_ids * capacity + slot_of
    dispatch_matrix = jnp.sum(
        (
            target[:, :, None] == jnp.arange(EXPERTS * capacity, dtype=jnp.int32)[None, None, :]
        ).astype(jnp.bfloat16),
        axis=1,
    )
    outgoing = jnp.einsum(
        "tr,td->rd", dispatch_matrix, normed, preferred_element_type=jnp.float32
    ).astype(jnp.bfloat16)
    outgoing = jnp.repeat(outgoing.reshape(EXPERTS, capacity, model_dim), shards, axis=0)
    arrived = lax.all_to_all(outgoing, "expert", split_axis=0, concat_axis=0, tiled=True)
    sources = arrived.shape[0]
    count = arrived.shape[1]
    flat_rows = arrived.reshape(sources * count, model_dim)
    gate = jnp.dot(flat_rows, gate_local, preferred_element_type=jnp.float32)
    upward = jnp.dot(flat_rows, up_local, preferred_element_type=jnp.float32)
    hidden = (jax.nn.silu(gate) * upward).astype(jnp.bfloat16)
    partial_out = jnp.dot(hidden, down_local, preferred_element_type=jnp.float32).astype(
        jnp.bfloat16
    )
    partials = partial_out.reshape(sources, count, model_dim)
    returned = lax.all_to_all(partials, "expert", split_axis=0, concat_axis=0, tiled=True)
    summed = jnp.sum(
        returned.astype(jnp.float32).reshape(EXPERTS, shards, capacity, model_dim), axis=1
    )
    picked = summed.reshape(EXPERTS * capacity, model_dim)[target]
    mixture = jnp.sum(weights_in[:, :, None] * picked, axis=1)
    layer_out = (widened + mixture).astype(jnp.bfloat16)
    handed = shifted(layer_out, "section", 1)
    return handed[None]


def solution(mesh):
    in_specs = (
        P("section", "expert", None),
        P("section", None),
        P("section", "expert", None),
        P("section", "expert", None),
        P("section", None, "expert"),
        P("section", None, "expert"),
        P("section", "expert", None),
    )
    out_specs = P("section", "expert", None)
    if mesh.shape["expert"] == EXPERTS:
        on_one = functools.partial(two_chips, mesh.shape["section"])
    else:
        on_one = on_device
    return jax.shard_map(
        on_one, mesh=mesh, in_specs=in_specs, out_specs=out_specs, check_vma=False
    )
```
